32 devices in a mesh: batch: 4 (over y, x), blk: 8 (over z, core).
Axes of the slice: x: 2, y: 2, z: 4, core: 2. Of those that a mesh axis runs over, the one named last changes fastest.
Arguments:
- tokens: bfloat16 [8, 1024, 1024], P('batch', 'blk'), may hold values from -6 to 6
- lengths: int32 [8, 4], P('batch'), may hold values from 1 to 1024, as said below
- ln1_gain: float32 [1024], replicated, may hold values from 0.25 to 1.75
- ln1_bias: float32 [1024], replicated, may hold values from -1.5 to 1.5
- w_qkv: bfloat16 [1024, 3072], replicated, may hold values from -0.1875 to 0.1875
- w_out: bfloat16 [1024, 1024], replicated, may hold values from -0.75 to 0.75
- ln2_gain: float32 [1024], replicated, may hold values from 0.25 to 1.75
- ln2_bias: float32 [1024], replicated, may hold values from -1.5 to 1.5
- w_up: bfloat16 [1024, 4096], replicated, may hold values from -0.1875 to 0.1875
- b_up: float32 [4096], replicated, may hold values from -2.5 to 2.5
- w_down: bfloat16 [4096, 1024], replicated, may hold values from -0.09375 to 0.09375
- b_down: float32 [1024], replicated, may hold values from -2.5 to 2.5
- cotangent: bfloat16 [8, 1024, 1024], P('batch', 'blk'), may hold values from -6 to 6
Outputs:
- output: bfloat16 [8, 1024, 1024], P('batch', 'blk')
- input_grad: bfloat16 [8, 1024, 1024], P('batch', 'blk')
- g_ln1_gain: float32 [1024], P('blk')
- g_ln1_bias: float32 [1024], P('blk')
- g_w_qkv: float32 [1024, 3072], P('blk')
- g_w_out: float32 [1024, 1024], P('blk')
- g_ln2_gain: float32 [1024], P('blk')
- g_ln2_bias: float32 [1024], P('blk')
- g_w_up: float32 [1024, 4096], P('blk')
- g_b_up: float32 [4096], P('blk')
- g_w_down: float32 [4096, 1024], P('blk')
- g_b_down: float32 [1024], P('blk')
The draws below stay inside these ranges and needn't reach their ends.
Inputs may be any that keep to these rules, and one draw needn't show every extreme that they name: In each row the 4 lengths are positive and sum to 1024.
All inputs are finite; a program needn't handle non-finite values.
Results may differ from the reference program's by a relative error of at most 0.035.
Values may be sent and summed in bfloat16 or wider, within the bound.
No kernel may reach another device: no remote copies, remote signals or barrier semaphores. Data moves between devices by JAX's collectives and lax.ppermute only.
A program may use at most 256 MiB of HBM per device.

```python
import math
import jax
import jax.numpy as jnp
from jax import lax

D = 1024
HEADS = 16
HEAD = 64
FF = 4096
TOK_DEV = 128
NSEG = 4
ROWS = 8
ROW_LEN = 1024


def draw_lengths(key, part):
    key = jax.random.fold_in(key, 7)
    first_key, tail_key = jax.random.split(key)
    first = jax.random.randint(first_key, (ROWS, 1), 1, TOK_DEV)
    tail = jax.random.randint(tail_key, (ROWS, NSEG - 2), 1, TOK_DEV // (NSEG - 2))
    middle = ROW_LEN - jnp.sum(first, 1, keepdims=True) - jnp.sum(tail, 1, keepdims=True)
    return jnp.concatenate([first, middle, tail], 1).astype(jnp.int32)


def level_of(key, extent, pieces, low, high):
    factor_of = 1.0
    for dim, blocks in pieces:
        steps = jax.random.uniform(jax.random.fold_in(jax.random.fold_in(key, 6), dim), (blocks,), jnp.float32, low / len(pieces), high / len(pieces))
        factor_of = factor_of * jnp.repeat(jnp.exp(steps), extent[dim] // blocks).reshape((-1,) + (1,) * (len(extent) - 1 - dim))
    return factor_of


def bell_draw(own_key, extent, deviation, reach, pieces=(), kind=jnp.bfloat16):
    array = deviation * jax.random.normal(own_key, extent, jnp.float32)
    if pieces:
        array = array * level_of(own_key, extent, pieces, -0.22, 0.18)
    return jnp.clip(array, -reach, reach).astype(kind)


def setup_inputs(seed: int = 0) -> dict:
    streams_of = jax.random.split(jax.random.key(seed), 14)
    tokens = bell_draw(streams_of[0], (ROWS, ROW_LEN, D), 1.0, 6.0, ((0, 4), (1, 8)))
    lengths = draw_lengths(jax.random.fold_in(streams_of[13], 71), 0)
    ln1_gain = jnp.clip(1.0 + 0.15 * jax.random.normal(streams_of[2], (D,), jnp.float32), 0.25, 1.75)
    ln1_bias = bell_draw(streams_of[3], (D,), 0.3, 1.5, (), jnp.float32)
    w_qkv = bell_draw(streams_of[4], (D, 3 * D), D ** -0.5, 0.1875)
    w_out = bell_draw(streams_of[5], (D, D), (D // 16) ** -0.5, 0.75)
    ln2_gain = jnp.clip(1.0 + 0.15 * jax.random.normal(streams_of[6], (D,), jnp.float32), 0.25, 1.75)
    ln2_bias = bell_draw(streams_of[7], (D,), 0.3, 1.5, (), jnp.float32)
    w_up = bell_draw(streams_of[8], (D, FF), D ** -0.5, 0.1875)
    b_up = bell_draw(streams_of[9], (FF,), 0.5, 2.5, (), jnp.float32)
    w_down = bell_draw(streams_of[10], (FF, D), FF ** -0.5, 0.09375)
    b_down = bell_draw(streams_of[11], (D,), 0.5, 2.5, (), jnp.float32)
    cotangent = bell_draw(streams_of[12], (ROWS, ROW_LEN, D), 1.0, 6.0, ((0, 4), (1, 8)))
    return {"tokens": tokens, "lengths": lengths, "ln1_gain": ln1_gain, "ln1_bias": ln1_bias, "w_qkv": w_qkv, "w_out": w_out, "ln2_gain": ln2_gain, "ln2_bias": ln2_bias, "w_up": w_up, "b_up": b_up, "w_down": w_down, "b_down": b_down, "cotangent": cotangent}


@jax.custom_vjp
def low(v):
    return lax.optimization_barrier(v.astype(jnp.bfloat16)).astype(jnp.float32)

@jax.custom_vjp
def low_back(v):
    return v

def low_keep(v):
    return (low(v), None)

def low_pass(kept, grad):
    return (grad,)

def back_keep(v):
    return (v, None)

def back_low(kept, grad):
    return (low(grad),)
low.defvjp(low_keep, low_pass)
low_back.defvjp(back_keep, back_low)
epsilon = 1e-05
masked = -1e+30

def matmul(left, right):
    return jnp.matmul(left, right, precision=lax.Precision.HIGHEST)

def layer_norm(values, gain, shift):
    mean = lax.optimization_barrier(jnp.mean(values, -1, keepdims=True))
    centred = values - mean
    spread = lax.optimization_barrier(jnp.mean(centred * centred, -1, keepdims=True))
    return centred * lax.rsqrt(spread + epsilon) * gain + shift

def segment_ids(row_lengths):
    ends = jnp.cumsum(row_lengths).astype(jnp.int32)
    places = jnp.arange(ROW_LEN, dtype=jnp.int32)
    return lax.optimization_barrier(jnp.sum((places[:, None] >= ends[None, :]).astype(jnp.int32), 1)).astype(jnp.int32)

def attend(query, keys, values, segment):
    block = math.gcd(ROW_LEN, 512)
    scale = HEAD ** (-0.5)
    key_place = jnp.arange(ROW_LEN, dtype=jnp.int32)

    def one_block(index):
        first = (index * block).astype(jnp.int32)
        rows = lax.dynamic_slice_in_dim(query, first, block, 0)
        place = first + jnp.arange(block, dtype=jnp.int32)
        own_seg = lax.dynamic_slice_in_dim(segment, first, block, 0)
        scores = low_back(jnp.einsum('qhd,khd->hqk', rows, keys, precision=lax.Precision.HIGHEST) * scale)
        allowed = (own_seg[:, None] == segment[None, :]) & (key_place[None, :] <= place[:, None])
        scores = jnp.where(allowed[None], scores, masked)
        top = lax.optimization_barrier(jnp.max(scores, -1, keepdims=True))
        weights = jnp.exp(scores - top)
        probs = weights / lax.optimization_barrier(jnp.sum(weights, -1, keepdims=True))
        return jnp.einsum('hqk,khd->qhd', low(probs), values, precision=lax.Precision.HIGHEST)
    blocks = lax.map(jax.checkpoint(one_block), jnp.arange(ROW_LEN // block, dtype=jnp.int32))
    return blocks.reshape(ROW_LEN, HEADS, HEAD)

def layer(inputs, ln1_gain, ln1_bias, w_qkv, w_out, ln2_gain, ln2_bias, w_up, b_up, w_down, b_down, segments):
    h_one = low(layer_norm(inputs, ln1_gain, ln1_bias))
    qkv = low(low_back(matmul(h_one, w_qkv)))
    query = qkv[:, :, :D].reshape(ROWS, ROW_LEN, HEADS, HEAD)
    keys = qkv[:, :, D:2 * D].reshape(ROWS, ROW_LEN, HEADS, HEAD)
    values = qkv[:, :, 2 * D:].reshape(ROWS, ROW_LEN, HEADS, HEAD)
    mixed = jax.vmap(attend)(query, keys, values, segments)
    attn = low(low_back(mixed.reshape(ROWS, ROW_LEN, D)))
    x_two = inputs + low_back(matmul(attn, w_out))
    h_two = low(layer_norm(x_two, ln2_gain, ln2_bias))
    hidden_pre = low_back(matmul(h_two, w_up) + b_up)
    active = low(jax.nn.gelu(hidden_pre, approximate=True))
    return x_two + low_back(matmul(active, w_down) + b_down)

def reference(tokens, lengths, ln1_gain, ln1_bias, w_qkv, w_out, ln2_gain, ln2_bias, w_up, b_up, w_down, b_down, cotangent):
    segments = jax.vmap(segment_ids)(lengths)
    params = (ln1_gain.astype(jnp.float32), ln1_bias.astype(jnp.float32), w_qkv.astype(jnp.float32), w_out.astype(jnp.float32), ln2_gain.astype(jnp.float32), ln2_bias.astype(jnp.float32), w_up.astype(jnp.float32), b_up.astype(jnp.float32), w_down.astype(jnp.float32), b_down.astype(jnp.float32))

    def forward(inputs, *weights):
        return layer(inputs, *weights, segments)
    result, pullback = jax.vjp(forward, tokens.astype(jnp.float32), *params)
    grads = pullback(cotangent.astype(jnp.float32))
    return (result.astype(jnp.bfloat16), grads[0].astype(jnp.bfloat16), grads[1], grads[2], grads[3], grads[4], grads[5], grads[6], grads[7], grads[8], grads[9], grads[10])
```

```python
import jax
import jax.numpy as jnp
from jax import lax
from jax.experimental import pallas as pl
from jax.experimental.pallas import tpu as pltpu
from jax.sharding import PartitionSpec as P

HEADS = 16
HEAD = 64
EPS = 1e-05
MASKED = -1e30
F32 = jnp.float32
BF16 = jnp.bfloat16


def dot(a, b, ca, cb):
    return lax.dot_general(a, b, (((ca,), (cb,)), ((), ())), preferred_element_type=F32)


def attend_kernel(heads, block, qkv_ref, start_ref, out_ref, lse_ref):
    frames = qkv_ref.shape[0]
    cols = heads * HEAD
    lane_head = lax.broadcasted_iota(jnp.int32, (1, cols), 1) // HEAD
    for qb in range(frames // block):
        first, end = qb * block, (qb + 1) * block
        q = qkv_ref[first:end, 0:cols] * jnp.asarray(HEAD**-0.5, BF16)
        k = qkv_ref[0:end, cols : 2 * cols]
        v = qkv_ref[0:end, 2 * cols : 3 * cols]
        start = start_ref[first:end, :]
        row = first + lax.broadcasted_iota(jnp.int32, (block, end), 0)
        col = lax.broadcasted_iota(jnp.int32, (block, end), 1)
        permit = (col <= row) & (col >= start)
        out = jnp.zeros((block, cols), F32)
        lses = []
        for h in range(heads):
            qh = jnp.where(lane_head == h, q, jnp.zeros_like(q))
            s = jnp.where(permit, dot(qh, k, 1, 1), MASKED)
            top = jnp.max(s, 1, keepdims=True)
            p = jnp.exp(s - top)
            total = jnp.sum(p, 1, keepdims=True)
            o = dot(p.astype(BF16), v, 1, 0) * (1.0 / total)
            out = jnp.where(lane_head == h, o, out)
            lses.append(top + jnp.log(total))
        out_ref[first:end, :] = out.astype(BF16)
        lane = lax.broadcasted_iota(jnp.int32, (block, 128), 1)
        lse = jnp.zeros((block, 128), F32)
        for h in range(heads):
            lse = jnp.where(lane == h, lses[h], lse)
        lse_ref[first:end, :] = lse


def attend(qkv, start, heads):
    frames = qkv.shape[0]
    return pl.pallas_call(
        lambda *refs: attend_kernel(heads, 256, *refs),
        out_shape=(
            jax.ShapeDtypeStruct((frames, heads * HEAD), BF16),
            jax.ShapeDtypeStruct((frames, 128), F32),
        ),
        compiler_params=pltpu.CompilerParams(vmem_limit_bytes=48 * 2**20),
        name="attend",
    )(qkv, start)


def attend_back_kernel(heads, block, qkv_ref, do_ref, stat_ref, start_ref, out_ref, dk_ref, dv_ref):
    frames = qkv_ref.shape[0]
    cols = heads * HEAD
    lane_head = lax.broadcasted_iota(jnp.int32, (1, cols), 1) // HEAD
    scale = HEAD**-0.5
    dk_ref[...] = jnp.zeros_like(dk_ref)
    dv_ref[...] = jnp.zeros_like(dv_ref)
    for qb in range(frames // block):
        first, end = qb * block, (qb + 1) * block
        q = qkv_ref[first:end, 0:cols] * jnp.asarray(scale, BF16)
        do = do_ref[first:end, :]
        k = qkv_ref[0:end, cols : 2 * cols]
        v = qkv_ref[0:end, 2 * cols : 3 * cols]
        start = start_ref[:, first:end]
        row = first + lax.broadcasted_iota(jnp.int32, (end, block), 1)
        col = lax.broadcasted_iota(jnp.int32, (end, block), 0)
        permit = (col <= row) & (col >= start)
        dq = jnp.zeros((block, cols), F32)
        for h in range(heads):
            qh = jnp.where(lane_head == h, q, jnp.zeros_like(q))
            doh = jnp.where(lane_head == h, do, jnp.zeros_like(do))
            s = dot(k, qh, 1, 1)
            p = jnp.where(permit, jnp.exp(s - stat_ref[h : h + 1, first:end]), 0.0)
            dp = dot(v, doh, 1, 1)
            ds = (p * (dp - stat_ref[heads + h : heads + h + 1, first:end])).astype(BF16)
            dv_ref[0:end, :] += dot(p.astype(BF16), doh, 1, 0)
            dk_ref[0:end, :] += dot(ds, qh, 1, 0)
            dq = jnp.where(lane_head == h, dot(ds, k, 0, 0), dq)
        out_ref[first:end, 0:cols] = (dq * scale).astype(BF16)
    out_ref[:, cols : 2 * cols] = dk_ref[...].astype(BF16)
    out_ref[:, 2 * cols : 3 * cols] = dv_ref[...].astype(BF16)


def attend_back(qkv, d_attn, stat, start, heads):
    frames = qkv.shape[0]
    return pl.pallas_call(
        lambda *refs: attend_back_kernel(heads, 256, *refs),
        out_shape=jax.ShapeDtypeStruct((frames, 3 * heads * HEAD), BF16),
        scratch_shapes=[
            pltpu.VMEM((frames, heads * HEAD), F32),
            pltpu.VMEM((frames, heads * HEAD), F32),
        ],
        compiler_params=pltpu.CompilerParams(vmem_limit_bytes=48 * 2**20),
        name="attend_back",
    )(qkv, d_attn, stat, start)


def feed_kernel(
    h_ref, g_ref, x_ref, wu_ref, bu_ref, wd_ref, bd_ref, gain_ref, wo_ref,
    act_ref, dpre_ref, out_ref, dx_ref, dy_ref, dattn_ref, gbu_ref, vec_ref,
    out_acc, dh_acc,
):
    step = pl.program_id(0)
    last = pl.num_programs(0) - 1
    h = h_ref[...]
    g = g_ref[...]
    pre = dot(h, wu_ref[...], 1, 0) + bu_ref[...]
    square = pre * pre
    t = jnp.tanh(pre * (0.7978845608 + (0.7978845608 * 0.044715) * square))
    half = 0.5 + 0.5 * t
    act = (pre * half).astype(BF16)
    slope = half + 0.5 * pre * (1.0 - t * t) * (0.7978845608 + (3 * 0.7978845608 * 0.044715) * square)
    d_pre = (dot(g, wd_ref[...], 1, 1) * slope).astype(BF16)
    act_ref[...] = act
    dpre_ref[...] = d_pre
    gbu_ref[...] = jnp.sum(d_pre.astype(F32), 0, keepdims=True)
    out_add = dot(act, wd_ref[...], 1, 0)
    dh_add = dot(d_pre, wu_ref[...], 1, 1)

    @pl.when(step == 0)
    def _():
        out_acc[...] = out_add
        dh_acc[...] = dh_add

    @pl.when(step > 0)
    def _():
        out_acc[...] += out_add
        dh_acc[...] += dh_add

    @pl.when(step == last)
    def _():
        x2 = x_ref[...]
        out_ref[...] = (x2 + out_acc[...] + bd_ref[...]).astype(BF16)
        mean = jnp.mean(x2, -1, keepdims=True)
        centred = x2 - mean
        inverse = lax.rsqrt(jnp.mean(centred * centred, -1, keepdims=True) + EPS)
        unit = centred * inverse
        dh = dh_acc[...]
        gf = g_ref[...].astype(F32)
        scaled = dh * gain_ref[...]
        dx = gf + inverse * (
            scaled
            - jnp.mean(scaled, -1, keepdims=True)
            - unit * jnp.mean(scaled * unit, -1, keepdims=True)
        )
        dx_ref[...] = dx
        dy = dx.astype(BF16)
        dy_ref[...] = dy
        dattn_ref[...] = dot(dy, wo_ref[...], 1, 1).astype(BF16)
        vec_ref[...] = jnp.zeros_like(vec_ref)
        vec_ref[0:1, :] = jnp.sum(dh * unit, 0, keepdims=True)
        vec_ref[1:2, :] = jnp.sum(dh, 0, keepdims=True)
        vec_ref[2:3, :] = jnp.sum(gf, 0, keepdims=True)


def feed(h2, g, x2, w_up, b_up, w_down, b_down, gain, w_out):
    tokens, width = h2.shape
    hidden = w_up.shape[1]
    span = 512
    whole = lambda i: (0, 0)
    return pl.pallas_call(
        feed_kernel,
        grid=(hidden // span,),
        in_specs=[
            pl.BlockSpec((tokens, width), whole),
            pl.BlockSpec((tokens, width), whole),
            pl.BlockSpec((tokens, width), whole),
            pl.BlockSpec((width, span), lambda i: (0, i)),
            pl.BlockSpec((1, span), lambda i: (0, i)),
            pl.BlockSpec((span, width), lambda i: (i, 0)),
            pl.BlockSpec((1, width), whole),
            pl.BlockSpec((1, width), whole),
            pl.BlockSpec((width, width), whole),
        ],
        out_specs=(
            pl.BlockSpec((tokens, span), lambda i: (0, i)),
            pl.BlockSpec((tokens, span), lambda i: (0, i)),
            pl.BlockSpec((tokens, width), whole),
            pl.BlockSpec((tokens, width), whole),
            pl.BlockSpec((tokens, width), whole),
            pl.BlockSpec((tokens, width), whole),
            pl.BlockSpec((1, span), lambda i: (0, i)),
            pl.BlockSpec((8, width), whole),
        ),
        out_shape=(
            jax.ShapeDtypeStruct((tokens, hidden), BF16),
            jax.ShapeDtypeStruct((tokens, hidden), BF16),
            jax.ShapeDtypeStruct((tokens, width), BF16),
            jax.ShapeDtypeStruct((tokens, width), F32),
            jax.ShapeDtypeStruct((tokens, width), BF16),
            jax.ShapeDtypeStruct((tokens, width), BF16),
            jax.ShapeDtypeStruct((1, hidden), F32),
            jax.ShapeDtypeStruct((8, width), F32),
        ),
        scratch_shapes=[
            pltpu.VMEM((tokens, width), F32),
            pltpu.VMEM((tokens, width), F32),
        ],
        compiler_params=pltpu.CompilerParams(vmem_limit_bytes=48 * 2**20),
        cost_estimate=pl.CostEstimate(
            flops=8 * tokens * width * hidden, bytes_accessed=4 * width * hidden, transcendentals=tokens * hidden
        ),
        name="feed",
    )(h2, g, x2, w_up, b_up[None], w_down, b_down[None], gain[None], w_out)


def layer_norm(values, gain, shift):
    mean = jnp.mean(values, -1, keepdims=True)
    centred = values - mean
    inverse = lax.rsqrt(jnp.mean(centred * centred, -1, keepdims=True) + EPS)
    unit = centred * inverse
    return unit * gain + shift, unit, inverse


def make(nb, nk):
    nz = nk // 2

    def on_device(
        tokens, lengths, ln1_gain, ln1_bias, w_qkv, w_out, ln2_gain, ln2_bias,
        w_up, b_up, w_down, b_down, cotangent,
    ):
        rows, frames, width = tokens.shape
        hidden = w_up.shape[1]
        group = nk // rows
        heads = HEADS // group
        cols = heads * HEAD
        whole_row = nk * frames
        own = rows * frames
        b = lax.axis_index("batch")
        k = lax.axis_index("blk")
        z, core = k // 2, k % 2
        hi, low = k // group, k % group

        def on_blk(v, mask):
            return lax.ppermute(v, "blk", [(i, i ^ mask) for i in range(nk)])

        def on_batch(v, mask):
            return lax.ppermute(v, "batch", [(i, i ^ mask) for i in range(nb)])

        def pick(v, index, axis=0):
            return lax.dynamic_index_in_dim(v, index, axis, keepdims=False)

        def pair_of(v):
            other = on_blk(pick(v, 1 - hi), group)
            mine = pick(v, hi)
            return jnp.where(hi == 0, jnp.stack([mine, other]), jnp.stack([other, mine]))

        def unpair(v):
            other = on_blk(pick(v, 1 - hi), group)
            mine = pick(v, hi)
            return jnp.where(hi == 0, jnp.stack([mine, other]), jnp.stack([other, mine]))

        def plane_gather(v):
            both = jnp.stack([v, on_blk(v, 1)])
            return jnp.stack([both] + [on_batch(both, m) for m in range(1, nb)])

        def plane_exchange(v):
            both = jnp.stack([pick(v, core, 1), on_blk(pick(v, 1 - core, 1), 1)], 1)
            return jnp.stack([pick(both, b)] + [on_batch(pick(both, b ^ m), m) for m in range(1, nb)])

        def line_sum(v):
            low_v = v.astype(BF16)
            total = pick(v, z)
            for m in range(1, nz):
                total = total + on_blk(pick(low_v, z ^ m), 2 * m).astype(F32)
            return total

        def batch_sum(v):
            low_v = v.astype(BF16)
            total = pick(v, b)
            for m in range(1, nb):
                total = total + on_batch(pick(low_v, b ^ m), m).astype(F32)
            return total

        def batch_gather(v):
            low_v = v.astype(BF16)
            out = jnp.zeros((nb,) + v.shape, F32)
            out = lax.dynamic_update_index_in_dim(out, low_v.astype(F32), b, 0)
            for m in range(1, nb):
                out = lax.dynamic_update_index_in_dim(out, on_batch(low_v, m).astype(F32), b ^ m, 0)
            return out

        def all_sum(v):
            m = 1
            while m < nk:
                v = v + on_blk(v, m)
                m *= 2
            m = 1
            while m < nb:
                v = v + on_batch(v, m)
                m *= 2
            return v

        pair = pair_of(tokens)
        rel = [pair]
        m = group // 2
        blocks = pair[None]
        bit = 1
        order = []
        held = {0: pair}
        m = group // 2
        while m >= 1:
            for key in list(held):
                held[key ^ m] = on_blk(held[key], m)
            m //= 2
        row_x = jnp.zeros((rows, group, frames, width), BF16)
        for key, v in held.items():
            row_x = lax.dynamic_update_slice_in_dim(row_x, v[:, None], low ^ key, 1)
        row_x = row_x.reshape(whole_row, width)

        cot_pair = pair_of(cotangent)
        g = cot_pair.reshape(own, width)
        g_all = plane_gather(g).reshape(nb * 2 * own, width)

        my_lengths = pick(lengths, hi)
        ends = jnp.cumsum(my_lengths)
        place = jnp.arange(whole_row, dtype=jnp.int32)
        start = jnp.sum(jnp.where(place[:, None] >= ends[None, :], my_lengths[None, :], 0), 1)

        def head_weights(which):
            parts = [
                lax.dynamic_slice_in_dim(w_qkv, i * width + which * cols, cols, 1) for i in range(3)
            ]
            return jnp.concatenate(parts, 1)

        w_mine = head_weights(low)
        h_row = layer_norm(row_x.astype(F32), ln1_gain, ln1_bias)[0].astype(BF16)
        qkv = dot(h_row, w_mine, 1, 0).astype(BF16)
        attn_heads, lse = attend(qkv, start[:, None], heads)

        pieces = attn_heads.reshape(rows, group, frames, cols)
        attn = jnp.zeros((rows, frames, group, cols), BF16)
        attn = lax.dynamic_update_slice_in_dim(attn, pick(pieces, low, 1)[:, :, None], low, 2)
        for m in range(1, group):
            got = on_blk(pick(pieces, low ^ m, 1), m)
            attn = lax.dynamic_update_slice_in_dim(attn, got[:, :, None], low ^ m, 2)
        attn = attn.reshape(own, width)

        x = pair.reshape(own, width).astype(F32)
        x2 = x + dot(attn, w_out, 1, 0)
        h2 = layer_norm(x2, ln2_gain, ln2_bias)[0].astype(BF16)
        act, d_pre, out, d_x2, d_y, d_attn, g_b_up, vec2 = feed(
            h2, g, x2, w_up, b_up, w_down, b_down, ln2_gain, w_out
        )

        pieces = d_attn.reshape(rows, frames, group, cols)
        d_heads = jnp.zeros((rows, group, frames, cols), BF16)
        d_heads = lax.dynamic_update_slice_in_dim(d_heads, pick(pieces, low, 2)[:, None], low, 1)
        for m in range(1, group):
            got = on_blk(pick(pieces, low ^ m, 2), m)
            d_heads = lax.dynamic_update_slice_in_dim(d_heads, got[:, None], low ^ m, 1)
        d_heads = d_heads.reshape(whole_row, cols)
        delta = jnp.sum(
            (d_heads.astype(F32) * attn_heads.astype(F32)).reshape(whole_row, heads, HEAD), -1
        )
        stat = jnp.concatenate([lse[:, :heads].T, delta.T], 0)
        stat = jnp.pad(stat, ((0, -2 * heads % 8), (0, 0)))
        d_qkv = attend_back(qkv, d_heads, stat, start[None, :], heads)

        halves = d_qkv.reshape(rows, group // 2, 2, frames, 3 * cols)
        mine = pick(halves, core, 2)
        other = on_blk(pick(halves, 1 - core, 2), 1)
        part = dot(mine.reshape(-1, 3 * cols), w_mine, 1, 1) + dot(
            other.reshape(-1, 3 * cols), head_weights(low ^ 1), 1, 1
        )
        part = part.reshape(rows, group // 2, frames, width)
        d_h1 = pick(part, low // 2, 1)
        part = part.astype(BF16)
        for m in range(1, group // 2):
            d_h1 = d_h1 + on_blk(pick(part, (low // 2) ^ m, 1), 2 * m).astype(F32)
        d_h1 = d_h1.reshape(own, width)
        _, unit, inverse = layer_norm(x, ln1_gain, ln1_bias)
        scaled = d_h1 * ln1_gain
        d_x = d_x2 + inverse * (
            scaled
            - jnp.mean(scaled, -1, keepdims=True)
            - unit * jnp.mean(scaled * unit, -1, keepdims=True)
        )
        input_grad = unpair(d_x.astype(BF16).reshape(rows, frames, width))
        output = unpair(out.reshape(rows, frames, width))

        tall = nb * 2 * own
        sub = hidden // nk // nb
        act_to = act.reshape(own, nz, 2, nb, sub).transpose(3, 2, 0, 1, 4).reshape(nb, 2, own, nz * sub)
        act_all = plane_exchange(act_to).reshape(tall, nz * sub)
        part = dot(act_all, g_all, 0, 0)
        g_w_down = batch_gather(line_sum(part.reshape(nz, sub, width))).reshape(nb * sub, width)

        h2_all = plane_gather(h2).reshape(tall, width)
        wide = hidden // nb // 2
        pre_to = d_pre.reshape(own, nb, 2, wide).transpose(1, 2, 0, 3)
        pre_all = plane_exchange(pre_to).reshape(tall, wide)
        part = dot(h2_all, pre_all, 0, 0).astype(BF16).reshape(nz, 2, width // nk, wide)
        mine = pick(part, core, 1)
        other = on_blk(pick(part, 1 - core, 1), 1)
        part = jnp.where(
            core == 0, jnp.concatenate([mine, other], 2), jnp.concatenate([other, mine], 2)
        )
        g_w_up = batch_gather(line_sum(part.astype(F32)))
        g_w_up = g_w_up.transpose(1, 0, 2).reshape(width // nk, hidden)

        sub = width // nk // nb
        part = dot(attn, d_y, 0, 0).reshape(nz, 2, nb, sub, width)
        mine = pick(part, core, 1) + on_blk(pick(part, 1 - core, 1).astype(BF16), 1).astype(F32)
        part = batch_sum(mine.transpose(1, 0, 2, 3))
        g_w_out = batch_gather(line_sum(part)).reshape(nb * sub, width)

        part = dot(h_row, d_qkv, 0, 0).reshape(nk, nb, sub, 3 * cols).transpose(1, 0, 2, 3)
        part = batch_sum(part)
        part = part.reshape(rows, group, sub, 3 * cols)
        part = pick(part, hi) + on_blk(pick(part, 1 - hi).astype(BF16), group).astype(F32)
        part = part.astype(BF16)
        full = jnp.zeros((sub, 3, group, cols), BF16)

        def place_cols(full, piece, index):
            return lax.dynamic_update_slice_in_dim(full, piece.reshape(sub, 3, 1, cols), index, 2)

        full = place_cols(full, pick(part, low), low)
        for m in range(1, group):
            full = place_cols(full, on_blk(pick(part, low ^ m), m), low ^ m)
        g_w_qkv = batch_gather(full.reshape(sub, 3 * width).astype(F32)).reshape(nb * sub, 3 * width)

        early = all_sum(jnp.concatenate([vec2[:3].reshape(3 * width // 128, 128), g_b_up.reshape(-1, 128)], 0))
        late = all_sum(jnp.concatenate([jnp.sum(d_h1 * unit, 0), jnp.sum(d_h1, 0)]).reshape(-1, 128))

        def share(v):
            v = v.reshape(-1)
            size = v.shape[0] // nk
            return lax.dynamic_slice_in_dim(v, k * size, size, 0)

        per = width // 128
        return (
            output,
            input_grad,
            share(late[:per]),
            share(late[per:]),
            g_w_qkv,
            g_w_out,
            share(early[:per]),
            share(early[per : 2 * per]),
            g_w_up,
            share(early[3 * per :]),
            g_w_down,
            share(early[2 * per : 3 * per]),
        )

    return on_device


def solution(mesh):
    vector = P()
    act = P("batch", "blk", None)
    return jax.shard_map(
        make(mesh.shape["batch"], mesh.shape["blk"]),
        mesh=mesh,
        in_specs=(act, P("batch", None)) + (vector,) * 10 + (act,),
        out_specs=(
            act, act, P("blk"), P("blk"), P("blk", None), P("blk", None), P("blk"), P("blk"),
            P("blk", None), P("blk"), P("blk", None), P("blk"),
        ),
        check_vma=False,
    )
```

```python
import jax
import jax.numpy as jnp
from jax import lax
from jax.experimental import pallas as pl
from jax.experimental.pallas import tpu as pltpu
from jax.sharding import PartitionSpec as P

HEADS = 16
HEAD = 64
EPS = 1e-05
MASKED = -1e30
F32 = jnp.float32
BF16 = jnp.bfloat16
SQ = 0.7978845608
CUBE = 0.044715
MIB = 2**20
HI, LOW, CORE, Z, B = range(5)

VMEM = pl.BlockSpec(memory_space=pltpu.VMEM)
SMEM = pl.BlockSpec(memory_space=pltpu.SMEM)
ANY = pl.BlockSpec(memory_space=pl.ANY)
MICROS = {
    "attend_rows": 11, "mix": 1.5, "feed": 10, "attend_back": 10.6, "qkv_grad": 2.5, "part": 3.4, "up_grad": 2.7,
    "down_grad": 2.6, "out_grad": 1.3, "place_up": 2, "place_down": 2, "place_qkv": 2, "place_out": 1.3,
}


def cost(name):
    return pl.CostEstimate(flops=int(1e10 * MICROS.get(name, 0.7)), bytes_accessed=0, transcendentals=0)


def dot(a, b, ca, cb):
    return lax.dot_general(a, b, (((ca,), (cb,)), ((), ())), preferred_element_type=F32)


def shape(dims, kind=BF16):
    return jax.ShapeDtypeStruct(tuple(dims), kind)


def call(body, outs, args, scalars=0, scratch=(), name=None, limit=48, deps=(), through=()):
    ins, count = len(args), len(outs)
    last = ins + len(deps) + len(through)
    done = last + count + len(through)
    return pl.pallas_call(
        lambda *refs: body(*refs[:ins], *refs[last : last + count], *refs[done:]),
        in_specs=[SMEM] * scalars + [VMEM] * (ins - scalars) + [ANY] * (len(deps) + len(through)),
        out_specs=tuple(VMEM for _ in outs) + tuple(ANY for _ in through),
        out_shape=tuple(outs) + tuple(shape(v.shape, v.dtype) for v in through),
        input_output_aliases={ins + len(deps) + i: count + i for i in range(len(through))},
        scratch_shapes=list(scratch),
        compiler_params=pltpu.CompilerParams(vmem_limit_bytes=limit * MIB),
        cost_estimate=cost(name),
        name=name,
    )(*args, *deps, *through)


def rows_at(index, size):
    return pl.ds(pl.multiple_of(index * size, size), size)


def normal(x):
    mean = jnp.mean(x, -1, keepdims=True)
    centred = x - mean
    inverse = lax.rsqrt(jnp.mean(centred * centred, -1, keepdims=True) + EPS)
    return centred * inverse, inverse


def normal_back(scaled, unit, inverse):
    return inverse * (
        scaled
        - jnp.mean(scaled, -1, keepdims=True)
        - unit * jnp.mean(scaled * unit, -1, keepdims=True)
    )


def starts(lengths_ref, hi, place):
    start = jnp.zeros_like(place)
    end = jnp.int32(0)
    for j in range(lengths_ref.shape[1]):
        size = lengths_ref[hi, j]
        end = end + size
        start = jnp.where(place >= end, end, start)
    return start


def attend_rows(heads, block, group, frames, meta, lengths, *refs):
    own, other = refs[:group], refs[group : 2 * group]
    w_ref, gain_ref, shift_ref = refs[2 * group : 2 * group + 3]
    h_ref, qkv_ref, attn_ref, lse_ref = refs[2 * group + 3 : 2 * group + 7]
    pieces = refs[2 * group + 7 :]
    hi, low = meta[HI], meta[LOW]
    cols = heads * HEAD
    total_rows = h_ref.shape[0]

    def place(kind, m):
        return rows_at((hi ^ kind) * group + (low ^ m), frames)

    for m in range(group):
        for kind, ref in ((0, own[m]), (1, other[m])):
            unit, _ = normal(ref[...].astype(F32))
            h_ref[place(kind, m), :] = (unit * gain_ref[...] + shift_ref[...]).astype(BF16)
    for r in range(0, total_rows, 256):
        qkv_ref[r : r + 256, :] = dot(h_ref[r : r + 256, :], w_ref[...], 1, 0).astype(BF16)
    lane_head = lax.broadcasted_iota(jnp.int32, (1, cols), 1) // HEAD
    for first in range(0, total_rows, block):
        end = first + block
        q = qkv_ref[first:end, 0:cols] * jnp.asarray(HEAD**-0.5, BF16)
        k = qkv_ref[0:end, cols : 2 * cols]
        v = qkv_ref[0:end, 2 * cols : 3 * cols]
        start = starts(lengths, hi, first + lax.broadcasted_iota(jnp.int32, (block, 1), 0))
        row = first + lax.broadcasted_iota(jnp.int32, (block, end), 0)
        col = lax.broadcasted_iota(jnp.int32, (block, end), 1)
        permit = (col <= row) & (col >= start)
        out = jnp.zeros((block, cols), F32)
        lane = lax.broadcasted_iota(jnp.int32, (block, 128), 1)
        lse = jnp.zeros((block, 128), F32)
        for h in range(heads):
            qh = jnp.where(lane_head == h, q, jnp.zeros_like(q))
            s = jnp.where(permit, dot(qh, k, 1, 1), MASKED)
            top = jnp.max(s, 1, keepdims=True)
            p = jnp.exp(s - top)
            total = jnp.sum(p, 1, keepdims=True)
            o = dot(p.astype(BF16), v, 1, 0) * (1.0 / total)
            out = jnp.where(lane_head == h, o, out)
            lse = jnp.where(lane == h, top + jnp.log(total), lse)
        attn_ref[first:end, :] = out.astype(BF16)
        lse_ref[:, first:end] = lse.T[: lse_ref.shape[0]]
    for m in range(group):
        for kind in (0, 1):
            pieces[m][kind * frames : (kind + 1) * frames, :] = attn_ref[place(kind, m), :]


def attend_back(heads, block, group, frames, meta, lengths, *refs):
    qkv_ref, attn_ref, lse_ref = refs[:3]
    pieces = refs[3 : 3 + group]
    full_ref, keep_ref, send_ref = refs[3 + group : 6 + group]
    do_ref, dk_ref, dv_ref, delta_ref = refs[6 + group :]
    hi, low, core = meta[HI], meta[LOW], meta[CORE]
    total_rows = qkv_ref.shape[0]
    cols = heads * HEAD
    for m in range(group):
        for kind in (0, 1):
            do_ref[rows_at((hi ^ kind) * group + (low ^ m), frames), :] = pieces[m][
                kind * frames : (kind + 1) * frames, :
            ]
    some = lse_ref.shape[0]
    pick = (
        lax.broadcasted_iota(jnp.int32, (some, cols), 1) // HEAD
        == lax.broadcasted_iota(jnp.int32, (some, cols), 0)
    ).astype(F32)
    for r in range(0, total_rows, block):
        product = do_ref[r : r + block, :].astype(F32) * attn_ref[r : r + block, :].astype(F32)
        delta_ref[:, r : r + block] = lax.dot_general(
            pick,
            product,
            (((1,), (1,)), ((), ())),
            precision=lax.Precision.HIGHEST,
            preferred_element_type=F32,
        )
    lane_head = lax.broadcasted_iota(jnp.int32, (1, cols), 1) // HEAD
    scale = HEAD**-0.5
    for first in reversed(range(0, total_rows, block)):
        end = first + block
        q = qkv_ref[first:end, 0:cols] * jnp.asarray(scale, BF16)
        do = do_ref[first:end, :]
        k = qkv_ref[0:end, cols : 2 * cols]
        v = qkv_ref[0:end, 2 * cols : 3 * cols]
        start = starts(lengths, hi, first + lax.broadcasted_iota(jnp.int32, (1, block), 1))
        row = first + lax.broadcasted_iota(jnp.int32, (end, block), 1)
        col = lax.broadcasted_iota(jnp.int32, (end, block), 0)
        permit = (col <= row) & (col >= start)
        dq = jnp.zeros((block, cols), F32)
        for h in range(heads):
            qh = jnp.where(lane_head == h, q, jnp.zeros_like(q))
            doh = jnp.where(lane_head == h, do, jnp.zeros_like(do))
            s = dot(k, qh, 1, 1)
            p = jnp.where(permit, jnp.exp(s - lse_ref[h : h + 1, first:end]), 0.0)
            dp = dot(v, doh, 1, 1)
            ds = (p * (dp - delta_ref[h : h + 1, first:end])).astype(BF16)
            dv = dot(p.astype(BF16), doh, 1, 0)
            dk = dot(ds, qh, 1, 0)
            if end == total_rows and h == 0:
                dv_ref[...] = dv
                dk_ref[...] = dk
            else:
                dv_ref[0:end, :] += dv
                dk_ref[0:end, :] += dk
            dq = jnp.where(lane_head == h, dot(ds, k, 0, 0), dq)
        full_ref[first:end, 0:cols] = (dq * scale).astype(BF16)
    full_ref[:, cols : 2 * cols] = dk_ref[...].astype(BF16)
    full_ref[:, 2 * cols : 3 * cols] = dv_ref[...].astype(BF16)
    for i in range(2 * group // 2):
        at = slice(i * frames, (i + 1) * frames)
        keep_ref[at, :] = full_ref[rows_at(2 * i + core, frames), :]
        send_ref[at, :] = full_ref[rows_at(2 * i + 1 - core, frames), :]


def mix(group, frames, meta, *refs):
    pieces = refs[:group]
    own_ref, other_ref, w_ref, gain_ref, shift_ref, x2_ref, h_ref = refs[group:]
    cols = pieces[0].shape[1]
    total = None
    for m in range(group):
        part = dot(pieces[m][...], w_ref[rows_at(meta[LOW] ^ m, cols), :], 1, 0)
        total = part if total is None else total + part
    for i, ref in enumerate((own_ref, other_ref)):
        at = slice(i * frames, (i + 1) * frames)
        x2 = ref[...].astype(F32) + total[at]
        x2_ref[at, :] = x2
        h_ref[at, :] = (normal(x2)[0] * gain_ref[...] + shift_ref[...]).astype(BF16)


def masks_without(nb, bit):
    return [m for m in range(nb) if not m & bit]


def split_store(b, bit, nb, tile, keep, send, j):
    masks = masks_without(nb, bit)
    for i in range(nb):
        mask = b ^ i
        low = lax.rem(mask, bit)
        index = low + lax.div(mask, 2 * bit) * bit

        @pl.when(mask & bit == 0)
        def _():
            keep[index, j] = tile(i)

        @pl.when(mask & bit != 0)
        def _():
            send[index, j] = tile(i)


def feed_body(part, parts, group, frames, nb, meta, *refs):
    h_ref, g_ref, wu_ref, bu_ref, wd_ref = refs[:5]
    refs = refs[5:]
    if part > 0:
        out_before, dh_before = refs[:2]
        refs = refs[2:]
    if part == parts - 1:
        x_ref, bd_ref, gain_ref, wo_ref = refs[:4]
        refs = refs[4:]
    act_keep, act_send, pre_keep, pre_send, gbu_ref = refs[:5]
    refs = refs[5:]
    out_acc, dh_acc = refs[-2:]
    step = pl.program_id(0)
    sub = act_keep.shape[3]
    pre = dot(h_ref[...], wu_ref[...], 1, 0) + bu_ref[...]
    square = pre * pre
    t = jnp.tanh(pre * (SQ + (SQ * CUBE) * square))
    half = 0.5 + 0.5 * t
    act = (pre * half).astype(BF16)
    slope = half + 0.5 * pre * (1.0 - t * t) * (SQ + (3 * SQ * CUBE) * square)
    d_pre = (dot(g_ref[...], wd_ref[...], 1, 1) * slope).astype(BF16)
    gbu_ref[...] = jnp.sum(d_pre.astype(F32), 0, keepdims=True)
    for v, bit, keep, send in ((act, 2, act_keep, act_send), (d_pre, 1, pre_keep, pre_send)):
        split_store(meta[B], bit, nb, lambda i: v[:, i * sub : (i + 1) * sub], keep, send, 0)
    out_add = dot(act, wd_ref[...], 1, 0)
    dh_add = dot(d_pre, wu_ref[...], 1, 1)

    @pl.when(step == 0)
    def _():
        if part > 0:
            out_acc[...] = out_before[...] + out_add
            dh_acc[...] = dh_before[...] + dh_add
        else:
            out_acc[...] = out_add
            dh_acc[...] = dh_add

    @pl.when(step > 0)
    def _():
        out_acc[...] += out_add
        dh_acc[...] += dh_add

    if part == parts - 1:
        out_keep, out_send, dx_ref, dy_ref = refs[:4]
        pieces, vec_ref = refs[4 : 4 + group], refs[4 + group]

        @pl.when(step == pl.num_programs(0) - 1)
        def _():
            x2 = x_ref[...]
            out = (x2 + out_acc[...] + bd_ref[...]).astype(BF16)
            out_keep[...] = out[:frames]
            out_send[...] = out[frames:]
            unit, inverse = normal(x2)
            dh = dh_acc[...]
            gf = g_ref[...].astype(F32)
            dx = gf + normal_back(dh * gain_ref[...], unit, inverse)
            dx_ref[...] = dx
            dy = dx.astype(BF16)
            dy_ref[...] = dy
            cols = pieces[0].shape[1]
            for m in range(group):
                pieces[m][...] = dot(dy, wo_ref[rows_at(meta[LOW] ^ m, cols), :], 1, 1).astype(BF16)
            vec_ref[...] = jnp.zeros_like(vec_ref)
            vec_ref[0:1, :] = jnp.sum(dh * unit, 0, keepdims=True)
            vec_ref[1:2, :] = jnp.sum(dh, 0, keepdims=True)
            vec_ref[2:3, :] = jnp.sum(gf, 0, keepdims=True)


def feed(part, parts, deps, before, meta, group, frames, nk, nb, h2, g, x2, w_up, b_up, w_down, b_down, gain, w_out):
    tokens, width = h2.shape
    hidden = w_up.shape[1]
    span = hidden // nk
    steps = nk // parts
    whole = lambda i, meta: (0, 0)
    last = part == parts - 1
    full = pl.BlockSpec((tokens, width), whole)
    row = pl.BlockSpec((1, width), whole)
    block = pl.BlockSpec((nb // 2, 1, tokens, span // nb), lambda i, meta: (0, i, 0, 0))
    args = [h2, g, w_up, b_up[None], w_down] + list(before)
    in_specs = [
        full,
        full,
        pl.BlockSpec((width, span), lambda i, meta: (0, parts * i + part)),
        pl.BlockSpec((1, span), lambda i, meta: (0, parts * i + part)),
        pl.BlockSpec((span, width), lambda i, meta: (parts * i + part, 0)),
    ] + [full] * len(before)
    out_shape = [shape((nb // 2, steps, tokens, span // nb))] * 4 + [shape((1, steps * span), F32)]
    out_specs = [block] * 4 + [pl.BlockSpec((1, span), lambda i, meta: (0, i))]
    scratch = []
    if last:
        args += [x2, b_down[None], gain[None], w_out]
        in_specs += [full, row, row, pl.BlockSpec((width, width), whole)]
        out_shape += [shape((frames, width))] * 2 + [shape((tokens, width), F32), shape((tokens, width))]
        out_shape += [shape((tokens, width // group))] * group + [shape((8, width), F32)]
        out_specs += [pl.BlockSpec((frames, width), whole)] * 2 + [full, full]
        out_specs += [pl.BlockSpec((tokens, width // group), whole)] * group
        out_specs += [pl.BlockSpec((8, width), whole)]
        scratch = [pltpu.VMEM((tokens, width), F32)] * 2
    else:
        out_shape += [shape((tokens, width), F32)] * 2
        out_specs += [full, full]
    ins = len(args) + 1
    return pl.pallas_call(
        lambda *refs: feed_body(part, parts, group, frames, nb, *refs[:ins], *refs[ins + len(deps) :]),
        grid_spec=pltpu.PrefetchScalarGridSpec(
            num_scalar_prefetch=1,
            grid=(steps,),
            in_specs=in_specs + [ANY] * len(deps),
            out_specs=out_specs,
            scratch_shapes=scratch,
        ),
        out_shape=out_shape,
        compiler_params=pltpu.CompilerParams(vmem_limit_bytes=48 * MIB),
        cost_estimate=cost("feed"),
        name="feed",
    )(meta, *args, *deps)


def side_by_side(ref, indices):
    return jnp.concatenate([ref[i, j] for i, j in indices], 1)


def hidden_body(nz, meta, *refs):
    pres, hs, acts, gs = refs[:2], refs[2:4], refs[4:6], refs[6:8]
    keep, send, acc = refs[8:]
    many, _, _, sub = pres[0].shape
    some = nz // 2
    tall, wide = keep.shape[3:]
    half = wide // 2
    width = acc.shape[0]
    core = meta[CORE]
    for i in range(2):
        order = [(r, z) for z in range(nz) for r in range(many)]
        part = dot(hs[i][...], side_by_side(pres[i], order), 0, 0)
        acc[...] = part if i == 0 else acc[...] + part
    rows = width // nz // 2
    for to, out in ((core, keep), (1 - core, send)):
        mine = acc[:, rows_at(to, some * many * sub)].astype(BF16)
        for r in range(many):
            v = jnp.concatenate([mine[:, (j * many + r) * sub : (j * many + r + 1) * sub] for j in range(some)], 1)
            for z in range(nz):
                for c in range(2):
                    first = (2 * z + c) * rows
                    out[0, r, z ^ meta[Z], :, rows_at(c ^ to, half)] = v[first : first + rows]
    for i in range(2):
        order = [(r, z) for r in range(many) for z in range(nz)]
        part = dot(side_by_side(acts[i], order), gs[i][...], 0, 0)
        acc[...] = part if i == 0 else acc[...] + part
    fold = tall // sub
    for to, out in ((core, keep), (1 - core, send)):
        for q in range(fold):
            v = acc[:, pl.ds(pl.multiple_of((to * fold + q) * wide, wide), wide)].astype(BF16)
            for r in range(many):
                for z in range(nz):
                    first = (r * nz + z) * sub
                    out[1, r, z ^ meta[Z], q * sub : (q + 1) * sub, :] = v[first : first + sub]


def hidden_cores(keep, got, *outs):
    many = keep.shape[1]
    for i in range(2):
        for r in range(many):
            outs[i * many + r][...] = (keep[i, r].astype(F32) + got[i, r].astype(F32)).astype(BF16)


def hidden_plane(count, *refs):
    ins, refs = refs[: 2 * count], refs[2 * count :]
    nz = ins[0].shape[0]
    more, outs = refs[:-nz], refs[-nz:]
    tall = ins[0].shape[1]
    for i in range(2):
        v = ins[i * count][...].astype(F32)
        for one in ins[i * count + 1 : (i + 1) * count]:
            v = v + one[...].astype(F32)
        for z, out in enumerate(outs):
            out[i * tall : (i + 1) * tall] = v[z].astype(BF16)
    if more:
        v = more[0][0].astype(F32) + more[1][0].astype(F32)
        v = v.astype(BF16).reshape(v.shape[0], 2, -1, ins[0].shape[2])
        small = v.shape[2]
        for z, out in enumerate(outs):
            for c in range(2):
                first = 2 * tall + c * small
                out[first : first + small] = v[z, c]


def sum_of(refs):
    v = refs[0][...].astype(F32)
    for one in refs[1:]:
        v = v + one[...].astype(F32)
    return v.astype(BF16)


def hidden_first(*refs):
    refs[-1][...] = sum_of(refs[:-1])


def hidden_line(meta, *refs):
    first, terms, outs = refs[0], refs[1:-4], refs[-4:]
    tall, wide = outs[0].shape
    half = wide // 2
    downs = []
    for h, v in enumerate((first[...], sum_of(terms))):
        outs[0][:, h * half : (h + 1) * half] = v[:tall, :half]
        outs[1][:, h * half : (h + 1) * half] = v[:tall, half:]
        downs.append(v[tall : 2 * tall])
    mine = meta[CORE] == 0
    outs[2][:tall] = jnp.where(mine, downs[0], downs[1])
    outs[3][:tall] = jnp.where(mine, downs[1], downs[0])
    small = (v.shape[0] - 2 * tall) // 2
    outs[2][tall:] = v[2 * tall : 2 * tall + small]
    outs[3][tall:] = v[2 * tall + small :]


def out_body(group, meta, *refs):
    pieces, dy_ref, keep, send = refs[:group], refs[group], refs[-2], refs[-1]
    nb, _, _, small, half = keep.shape
    for core, out in ((meta[CORE], keep), (1 - meta[CORE], send)):
        dy = dy_ref[:, rows_at(core, half)]
        for m in range(group):
            part = dot(pieces[m][...], dy, 0, 0).astype(BF16)
            for j in range(2):
                for i in range(nb):
                    first = (j * nb + i) * small
                    at = (meta[B] ^ i, meta[LOW] ^ m ^ meta[Z], j ^ core)
                    out[at] = part[first : first + small]


def reverse_bits(v, count):
    out = 0
    for j in range(count):
        out = out + ((v >> j) & 1) * 2 ** (count - 1 - j)
    return out


def qkv_body(meta, h_ref, d_ref, keep, send, acc):
    half, nk, small, _ = keep.shape
    nb = 2 * half
    acc[...] = dot(h_ref[...], d_ref[...], 0, 0)
    for i in range(nb):
        index = reverse_bits(meta[B] ^ i, nb.bit_length() - 1)
        for out, mine in ((keep, index < half), (send, index >= half)):

            @pl.when(mine)
            def _():
                for j in range(nk):
                    first = (j * nb + i) * small
                    out[lax.rem(index, half), j] = acc[first : first + small, :].astype(BF16)


def fold_body(keep, ref, *outs):
    count = ref.shape[0] // keep
    v = ref[:keep].astype(F32)
    for i in range(1, count):
        v = v + ref[i * keep : (i + 1) * keep].astype(F32)
    v = v.astype(BF16)
    for out in outs:
        if len(out.shape) == len(v.shape):
            out[...] = v
        else:
            for i in range(out.shape[0]):
                out[i] = v


def add_body(count, cuts, *refs):
    ins, outs = refs[:count], refs[count:]
    first = 0
    for out, size in zip(outs, cuts):
        v = ins[0][first : first + size].astype(F32)
        for one in ins[1:]:
            v = v + one[first : first + size].astype(F32)
        out[...] = v.astype(out.dtype).reshape(out.shape)
        first = first + size


def stack_body(*refs):
    at = 0
    for ref in refs[:-1]:
        size = ref.shape[0]
        refs[-1][at : at + size] = ref[...]
        at += size


def part_body(group, frames, meta, keep_ref, got_ref, mine_ref, theirs_ref, *refs):
    outs, acc = refs[:-1], refs[-1]
    acc[...] = dot(keep_ref[...], mine_ref[...], 1, 1) + dot(got_ref[...], theirs_ref[...], 1, 1)
    half = group // 2
    for m in range(half):
        for kind in (0, 1):
            first = (meta[HI] ^ kind) * half + (lax.div(meta[LOW], 2) ^ m)
            outs[m][kind * frames : (kind + 1) * frames, :] = acc[rows_at(first, frames), :].astype(
                outs[m].dtype
            )


def final_body(frames, count, *refs):
    terms = refs[:count]
    own_ref, other_ref, dx_ref, gain_ref, keep_ref, send_ref, vec_ref = refs[count:]
    gains = jnp.zeros((1, dx_ref.shape[1]), F32)
    sums = gains
    for i, (ref, out) in enumerate(((own_ref, keep_ref), (other_ref, send_ref))):
        at = slice(i * frames, (i + 1) * frames)
        dh = terms[0][at, :]
        for term in terms[1:]:
            dh = dh + term[at, :].astype(F32)
        unit, inverse = normal(ref[...].astype(F32))
        out[...] = (dx_ref[at, :] + normal_back(dh * gain_ref[...], unit, inverse)).astype(BF16)
        gains = gains + jnp.sum(dh * unit, 0, keepdims=True)
        sums = sums + jnp.sum(dh, 0, keepdims=True)
    vec_ref[...] = jnp.zeros_like(vec_ref)
    vec_ref[0:1, :] = gains
    vec_ref[1:2, :] = sums


def place_down(tall, fold, masks, meta, *refs):
    pieces, out, more = refs[:-2], refs[-2], refs[-1]
    at = 0
    for ref in pieces:
        for i in range(ref.shape[0]):
            rows, cols = tall // fold, ref.shape[3]
            small = ref.shape[2] - tall
            for c in range(2):
                more[rows_at(meta[B] ^ masks[at], small), rows_at(c ^ meta[CORE], cols)] = ref[i, c, tall:].astype(F32)
                for q in range(fold):
                    out[rows_at(meta[B] ^ masks[at], rows), rows_at((c ^ meta[CORE]) * fold + q, cols)] = ref[
                        i, c, q * rows : (q + 1) * rows
                    ].astype(F32)
            at += 1


def place_up(nb, nz, masks, meta, *refs):
    pieces, out = refs[:-1], refs[-1]
    at = 0
    for ref in pieces:
        for i in range(ref.shape[0]):
            some = nz // 2
            sub = ref.shape[3] // nz
            for c in range(2):
                for h in range(2):
                    for j in range(some):
                        chip = (c ^ meta[CORE]) * some + j
                        first = (2 * chip + h) * nb + (meta[B] ^ masks[at])
                        lane = (h * some + j) * sub
                        out[:, rows_at(first, sub)] = ref[i, c, :, lane : lane + sub].astype(F32)
            at += 1


def place_qkv(ref, out):
    nb, group, small, width = ref.shape
    cols = width // 3
    for i in range(nb):
        for l in range(group):
            for j in range(3):
                first = (j * group + l) * cols
                out[i * small : (i + 1) * small, first : first + cols] = ref[
                    i, l, :, j * cols : (j + 1) * cols
                ].astype(F32)


def make(nb, nk):
    nz = nk // 2

    def on_blk(v, mask):
        return lax.ppermute(v, "blk", [(i, i ^ mask) for i in range(nk)])

    def on_batch(v, mask):
        return lax.ppermute(v, "batch", [(i, i ^ mask) for i in range(nb)])

    def on_device(
        tokens, lengths, ln1_gain, ln1_bias, w_qkv, w_out, ln2_gain, ln2_bias,
        w_up, b_up, w_down, b_down, cotangent,
    ):
        _, frames, width = tokens.shape
        hidden = w_up.shape[1]
        group = nk // 2
        heads = HEADS // group
        cols = heads * HEAD
        whole_row = nk * frames
        own = 2 * frames
        some = -(-heads // 8) * 8
        b = lax.axis_index("batch")
        k = lax.axis_index("blk")
        z, core = k // 2, k % 2
        hi, low = k // group, k % group
        meta = jnp.stack([hi, low, core, z, b, b, b, b]).astype(jnp.int32)

        def pick(v, index):
            return lax.dynamic_index_in_dim(v, index, 0, keepdims=False)

        before = []

        def kernel(body, outs, args, *rest, deps=(), **kw):
            result = call(body, outs, args, *rest, deps=list(deps) + before, **kw)
            before[:] = [min(result[: len(outs)], key=lambda v: v.size)]
            return result

        mine = {0: pick(tokens, hi)}
        other = {0: on_blk(pick(tokens, 1 - hi), group)}
        def choose(meta, v, keep, send):
            keep[...] = v[meta[HI]]
            send[...] = v[1 - meta[HI]]

        cot_mine, cot_send = kernel(
            choose,
            [shape((frames, width))] * 2,
            [meta, cotangent],
            1,
            deps=[other[0]],
            name="cotangent",
        )
        m = group // 2
        while m >= 1:
            for v in (mine, other):
                for key in list(v):
                    v[key ^ m] = on_blk(v[key], m)
            m //= 2
        mine = [mine[m] for m in range(group)]
        other = [other[m] for m in range(group)]

        def head_weights(which):
            parts = [
                lax.dynamic_slice_in_dim(w_qkv, i * width + which * cols, cols, 1) for i in range(3)
            ]
            return jnp.concatenate(parts, 1)

        w_mine, w_theirs = head_weights(low), head_weights(low ^ 1)

        h_row, qkv, attn_heads, lse, *pieces = kernel(
            lambda *refs: attend_rows(heads, 256, group, frames, *refs),
            [
                shape((whole_row, width)),
                shape((whole_row, 3 * cols)),
                shape((whole_row, cols)),
                shape((some, whole_row), F32),
            ]
            + [shape((own, cols))] * group,
            [meta, lengths] + mine + other + [w_mine, ln1_gain[None], ln1_bias[None]],
            scalars=2,
            name="attend_rows",
        )
        attn = [pieces[0]] + [on_blk(pieces[m], m) for m in range(1, group)]

        def join(a, c, out):
            out[:frames] = a[...]
            out[frames:] = c[...]

        (g,) = kernel(join, [shape((own, width))], [cot_mine, on_blk(cot_send, group)], name="join")
        g_other = on_batch(g, 2)
        x2, h2 = kernel(
            lambda *refs: mix(group, frames, *refs),
            [shape((own, width), F32), shape((own, width))],
            [meta] + attn + [mine[0], other[0], w_out, ln2_gain[None], ln2_bias[None]],
            scalars=1,
            name="mix",
        )
        h2_other = on_batch(h2, 1)
        feed_args = (meta, group, frames, nk, nb, h2, g, x2, w_up, b_up, w_down, b_down, ln2_gain, w_out)
        act_keep, act_send, pre_keep, pre_send, gbu_0, *rest = feed(0, 2, before + [g_other], (), *feed_args)
        hidden_0 = [pre_keep, on_batch(pre_send, 1), h2, h2_other, act_keep, on_batch(act_send, 2), g, g_other]
        act_keep, act_send, pre_keep, pre_send, gbu_1, out_keep, out_send, d_x2, d_y, *rest = feed(
            1, 2, [h2_other], rest, *feed_args
        )
        pieces, vec2 = rest[:group], rest[group]
        before[:] = [vec2]
        d_heads = [pieces[0]] + [on_blk(pieces[m], m) for m in range(1, group)]
        hidden_1 = [pre_keep, on_batch(pre_send, 1), h2, h2_other, act_keep, on_batch(act_send, 2), g, g_other]

        rows = width // nk
        small = rows // nb
        sub = hidden // nk // nb
        half = width // 2
        simple = small % 8 == 0 and sub % 128 == 0 and cols % 128 == 0
        bits = [2**j for j in range(nb.bit_length() - 1)]

        def add(arrays, cuts, drop=True, name="add", deps=()):
            rest = arrays[0].shape[1:]
            outs = [shape(rest if size == 1 and drop else (size,) + rest) for size in cuts]
            return kernel(lambda *refs: add_body(len(arrays), cuts, *refs), outs, list(arrays), name=name, deps=deps)

        def plane(v):
            return lax.all_to_all(v, "batch", 0, 0, tiled=True)

        def line(v):
            return lax.all_to_all(v, "blk", 0, 0, tiled=True)

        wide = hidden // 2 // nb

        def hidden_grad(args):
            keep, send = kernel(
                lambda *refs: hidden_body(nz, *refs),
                [shape((2, nb // 2, nz, rows, wide))] * 2,
                [meta] + args,
                scalars=1,
                scratch=[pltpu.VMEM((width, width), F32)],
                name="hidden_grad",
            )
            return keep, on_blk(send, 1)

        def hidden_cores_sum(keep, got, **kw):
            parts = kernel(hidden_cores, [shape((nz, rows, wide))] * nb, [keep, got], name="hidden_cores", **kw)
            half = nb // 2
            ups = [on_batch(v, m) for v, m in zip(parts[1:half], masks_without(nb, 1)[1:])]
            downs = [on_batch(v, m) for v, m in zip(parts[half + 1 :], masks_without(nb, 2)[1:])]
            return [parts[0]] + ups + [parts[half]] + downs

        extra = small * half // wide

        def hidden_plane_sum(terms, more=()):
            tall = 2 * rows + (2 * extra if more else 0)
            parts = kernel(
                lambda *refs: hidden_plane(nb // 2, *refs),
                [shape((tall, wide))] * nz,
                list(terms) + list(more),
                name="hidden_plane",
            )
            return [parts[0]] + [on_blk(parts[m], 2 * m) for m in range(1, nz)]

        if simple:
            keep_out, send_out = kernel(
                lambda *refs: out_body(group, *refs),
                [shape((nb, nz, 2, small, half))] * 2,
                [meta] + attn + [d_y],
                scalars=1,
                name="out_grad",
            )
        else:
            w = jnp.stack([dot(one, d_y, 0, 0) for one in attn]).astype(BF16)[low ^ jnp.arange(group)]
            w = w.reshape(nz, 2, nb, small, 2, half).transpose(4, 2, 0, 1, 3, 5)
            w = w[core ^ jnp.arange(2)][:, b ^ jnp.arange(nb)][:, :, z ^ jnp.arange(nz)]
            w = w[:, :, :, core ^ jnp.arange(2)]
            keep_out, send_out = w[0], w[1][:, :, ::-1]

        def out_halve(keep, got, deps=()):
            size = keep.shape[0]
            return add([keep, got], [size // 2, size // 2], drop=False, name="out_sum", deps=deps)

        hidden_0 = hidden_grad(hidden_0)
        out_got = on_blk(send_out, 1)
        hidden_0 = hidden_cores_sum(*hidden_0, deps=d_heads[1:] + [out_got])
        out_keep2, out_send2 = out_halve(keep_out, out_got)
        out_got = on_batch(out_send2, bits[-1])
        hidden_1 = hidden_grad(hidden_1)
        hidden_1 = hidden_cores_sum(*hidden_1)
        hidden_0 = hidden_plane_sum(hidden_0)
        for mask in bits[-2::-1]:
            out_keep2, out_send2 = out_halve(out_keep2, out_got)
            out_got = on_batch(out_send2, mask)
        d_qkv, keep, send = kernel(
            lambda *refs: attend_back(heads, 256, group, frames, *refs),
            [shape((whole_row, 3 * cols))] + [shape((whole_row // 2, 3 * cols))] * 2,
            [meta, lengths, qkv, attn_heads, lse] + d_heads,
            scalars=2,
            scratch=[
                pltpu.VMEM((whole_row, cols), BF16),
                pltpu.VMEM((whole_row, cols), F32),
                pltpu.VMEM((whole_row, cols), F32),
                pltpu.VMEM((some, whole_row), F32),
            ],
            name="attend_back",
        )
        got = on_blk(send, 1)
        if simple:
            qkv_keep, qkv_send = kernel(
                qkv_body,
                [shape((nb // 2, nk, small, 3 * cols))] * 2,
                [meta, h_row, d_qkv],
                scalars=1,
                scratch=[pltpu.VMEM((width, 3 * cols), F32)],
                name="qkv_grad",
            )
        else:
            w = dot(h_row, d_qkv, 0, 0).astype(BF16).reshape(nk, nb, small, 3 * cols)
            order = [reverse_bits(i, len(bits)) for i in range(nb)]
            w = w[:, b ^ jnp.array(order)].transpose(1, 0, 2, 3)
            qkv_keep, qkv_send = w[: nb // 2], w[nb // 2 :]

        qkv_got = on_batch(qkv_send, bits[0])
        hidden_1 = hidden_plane_sum(hidden_1, [out_keep2, out_got])
        terms = kernel(
            lambda *refs: part_body(group, frames, *refs),
            [shape((own, width), F32)] + [shape((own, width))] * (group // 2 - 1),
            [meta, keep, got, w_mine, w_theirs],
            scalars=1,
            scratch=[pltpu.VMEM((whole_row // 2, width), F32)],
            name="part",
        )
        terms = [terms[0]] + [on_blk(terms[m], 2 * m) for m in range(1, group // 2)]
        (first,) = kernel(hidden_first, [shape((2 * rows, wide))], hidden_0, name="hidden_first", deps=[qkv_got])

        def halve(keep, got):
            size = keep.shape[0]
            if size == 1:
                return add([keep, got], [1], name="qkv_sum")
            return add([keep, got], [size // 2, size // 2], drop=False, name="qkv_sum")

        for mask in bits[1:]:
            qkv_keep, qkv_send = halve(qkv_keep, qkv_got)
            qkv_got = on_batch(qkv_send, mask)
        keep, send, vec1 = kernel(
            lambda *refs: final_body(frames, len(terms), *refs),
            [shape((frames, width))] * 2 + [shape((8, width), F32)],
            list(terms) + [mine[0], other[0], d_x2, ln1_gain[None]],
            name="final",
            deps=[qkv_got],
        )
        (part,) = halve(qkv_keep, qkv_got)
        part = line(part)
        up_keep, up_send, down_keep, down_send = kernel(
            hidden_line,
            [shape((rows, wide))] * 2 + [shape((rows + extra, wide))] * 2,
            [meta, first] + hidden_1,
            1,
            name="hidden_line",
        )
        up_got, down_got = on_blk(up_send, 1), on_blk(down_send, 1)

        def pair_up(meta, keep, got, out):
            out[meta[HI]] = keep[...]
            out[1 - meta[HI]] = got[...]

        def two_rows(keep, got):
            (v,) = kernel(pair_up, [shape((2, frames, width))], [meta, keep, got], 1, name="pair")
            return v

        grad_got = on_blk(send, group)
        grad_keep = keep
        v = jnp.concatenate(
            [vec1[:2].reshape(-1, 128), vec2[:3].reshape(-1, 128)]
            + [gbu_0.reshape(-1, 128), gbu_1.reshape(-1, 128)],
            0,
        )
        masks = [(on_blk, 2**j) for j in range(nk.bit_length() - 1)] + [(on_batch, m) for m in bits]

        def vec_move(v):
            move, mask = masks.pop(0)
            return move(v, mask)

        def vec_add(v, got, **kw):
            (v,) = kernel(
                lambda *refs: add_body(2, [v.shape[0]], *refs), [shape(v.shape, F32)], [v, got], name="vec", **kw
            )
            return v

        def stack(pieces, deps=()):
            if len(pieces) == 1:
                return pieces[0]
            size = sum(one.shape[0] for one in pieces)
            (v,) = kernel(
                stack_body, [shape((size,) + pieces[0].shape[1:])], list(pieces), name="stack", deps=deps
            )
            return v

        vec_got = vec_move(v)
        up = [stack([up_keep[None], up_got[None]], deps=[down_got, vec_got])[None]]
        down = [stack([down_keep[None], down_got[None]])[None]]
        v = vec_add(v, vec_got)
        up_order, down_order = [0], [0]
        for mask_up, mask_down in zip(bits, bits[::-1]):
            vec_got = vec_move(v)
            if len(up_order) > 1:
                up = [stack(up, deps=[down[-1], vec_got])]
                down = [stack(down)]
                v = vec_add(v, vec_got)
            up, up_order = [up[0], on_batch(up[0], mask_up)], up_order + [mask_up ^ one for one in up_order]
            down, down_order = (
                [down[0], on_batch(down[0], mask_down)],
                down_order + [mask_down ^ one for one in down_order],
            )
            if len(up_order) == 2:
                (qkvs,) = kernel(
                    lambda *refs: fold_body(group, *refs),
                    [shape((nb, group, small, 3 * cols))],
                    [part],
                    name="qkv_line",
                    deps=[vec_got],
                )
                qkvs = plane(qkvs)
                v = vec_add(v, vec_got)
        while masks:
            v = vec_add(v, vec_move(v))
        input_grad = two_rows(grad_keep, grad_got)
        output = two_rows(out_keep, on_blk(out_send, group))

        if simple:
            (g_w_up,) = kernel(
                lambda *refs: place_up(nb, nz, up_order, *refs),
                [shape((rows, hidden), F32)],
                [meta] + up,
                1,
                name="place_up",
            )
            g_w_down, g_w_out = kernel(
                lambda *refs: place_down(rows, rows // sub, down_order, *refs),
                [shape((nb * sub, width), F32), shape((rows, width), F32)],
                [meta] + down,
                1,
                name="place_down",
            )
            (g_w_qkv,) = kernel(place_qkv, [shape((rows, 3 * width), F32)], [qkvs], name="place_qkv")
        else:
            both = core ^ jnp.arange(2)

            def in_order(pieces, order):
                back = [order.index(i) for i in range(nb)]
                w = jnp.concatenate(pieces, 0)[jnp.array(back)]
                return w[b ^ jnp.arange(nb)].astype(F32)

            more = in_order(down, down_order)[:, both]
            w = more[:, :, :rows].reshape(nb, 2, rows // sub, sub, wide)
            g_w_down = w.transpose(0, 3, 1, 2, 4).reshape(nb * sub, width)
            w = more[:, :, rows:].reshape(nb, 2, small, half)
            g_w_out = w.transpose(0, 2, 1, 3).reshape(rows, width)
            w = in_order(up, up_order)[:, both].reshape(nb, 2, rows, 2, nz // 2, sub)
            g_w_up = w.transpose(2, 1, 4, 3, 0, 5).reshape(rows, hidden)
            w = qkvs.reshape(nb, group, small, 3, cols).transpose(0, 2, 3, 1, 4)
            g_w_qkv = w.reshape(rows, 3 * width).astype(F32)

        per = width // 128

        def share(first, count):
            flat = v[first : first + count].reshape(-1)
            if first == 5 * per:
                flat = flat.reshape(2, nz, -1).transpose(1, 0, 2).reshape(-1)
            size = flat.shape[0] // nk
            return lax.dynamic_slice_in_dim(flat, k * size, size, 0)

        return (
            output,
            input_grad,
            share(0, per),
            share(per, per),
            g_w_qkv,
            g_w_out,
            share(2 * per, per),
            share(3 * per, per),
            g_w_up,
            share(5 * per, hidden // 128),
            g_w_down,
            share(4 * per, per),
        )

    return on_device


def solution(mesh):
    act = P("batch", "blk", None)
    return jax.shard_map(
        make(mesh.shape["batch"], mesh.shape["blk"]),
        mesh=mesh,
        in_specs=(act, P("batch", None)) + (P(),) * 10 + (act,),
        out_specs=(
            act, act, P("blk"), P("blk"), P("blk", None), P("blk", None), P("blk"), P("blk"),
            P("blk", None), P("blk"), P("blk", None), P("blk"),
        ),
        check_vma=False,
    )
```

```python
import jax
import jax.numpy as jnp
from jax import lax
from jax.experimental import pallas as pl
from jax.experimental.pallas import tpu as pltpu
from jax.sharding import PartitionSpec as P

HEADS = 16
HEAD = 64
EPS = 1e-05
MASKED = -1e30
F32 = jnp.float32
BF16 = jnp.bfloat16
SQ = 0.7978845608
CUBE = 0.044715
MIB = 2**20
HI, LOW, CORE, Z, B = range(5)

VMEM = pl.BlockSpec(memory_space=pltpu.VMEM)
SMEM = pl.BlockSpec(memory_space=pltpu.SMEM)
ANY = pl.BlockSpec(memory_space=pl.ANY)
MICROS = {
    "attend_rows": 11, "mix": 1.5, "feed": 10, "attend_back": 10.6, "qkv_grad": 2.5, "part": 3.4, "up_grad": 2.7,
    "down_grad": 2.6, "out_grad": 1.3, "place_up": 2, "place_down": 2, "place_qkv": 2, "place_out": 1.3,
}


def cost(name):
    return pl.CostEstimate(flops=int(1e10 * MICROS.get(name, 0.7)), bytes_accessed=0, transcendentals=0)


def dot(a, b, ca, cb):
    return lax.dot_general(a, b, (((ca,), (cb,)), ((), ())), preferred_element_type=F32)


def shape(dims, kind=BF16):
    return jax.ShapeDtypeStruct(tuple(dims), kind)


def call(body, outs, args, scalars=0, scratch=(), name=None, limit=48, deps=(), through=()):
    ins, count = len(args), len(outs)
    last = ins + len(deps) + len(through)
    done = last + count + len(through)
    return pl.pallas_call(
        lambda *refs: body(*refs[:ins], *refs[last : last + count], *refs[done:]),
        in_specs=[SMEM] * scalars + [VMEM] * (ins - scalars) + [ANY] * (len(deps) + len(through)),
        out_specs=tuple(VMEM for _ in outs) + tuple(ANY for _ in through),
        out_shape=tuple(outs) + tuple(shape(v.shape, v.dtype) for v in through),
        input_output_aliases={ins + len(deps) + i: count + i for i in range(len(through))},
        scratch_shapes=list(scratch),
        compiler_params=pltpu.CompilerParams(vmem_limit_bytes=limit * MIB),
        cost_estimate=cost(name),
        name=name,
    )(*args, *deps, *through)


def rows_at(index, size):
    return pl.ds(pl.multiple_of(index * size, size), size)


def normal(x):
    mean = jnp.mean(x, -1, keepdims=True)
    centred = x - mean
    inverse = lax.rsqrt(jnp.mean(centred * centred, -1, keepdims=True) + EPS)
    return centred * inverse, inverse


def normal_back(scaled, unit, inverse):
    return inverse * (
        scaled
        - jnp.mean(scaled, -1, keepdims=True)
        - unit * jnp.mean(scaled * unit, -1, keepdims=True)
    )


def starts(lengths_ref, hi, place):
    start = jnp.zeros_like(place)
    end = jnp.int32(0)
    for j in range(lengths_ref.shape[1]):
        size = lengths_ref[hi, j]
        end = end + size
        start = jnp.where(place >= end, end, start)
    return start


def attend_rows(heads, block, group, frames, meta, lengths, *refs):
    own, other = refs[:group], refs[group : 2 * group]
    w_ref, gain_ref, shift_ref = refs[2 * group : 2 * group + 3]
    h_ref, qkv_ref, attn_ref, lse_ref = refs[2 * group + 3 : 2 * group + 7]
    pieces = refs[2 * group + 7 :]
    hi, low = meta[HI], meta[LOW]
    cols = heads * HEAD
    total_rows = h_ref.shape[0]

    def place(kind, m):
        return rows_at((hi ^ kind) * group + (low ^ m), frames)

    for m in range(group):
        for kind, ref in ((0, own[m]), (1, other[m])):
            unit, _ = normal(ref[...].astype(F32))
            h_ref[place(kind, m), :] = (unit * gain_ref[...] + shift_ref[...]).astype(BF16)
    for r in range(0, total_rows, 256):
        qkv_ref[r : r + 256, :] = dot(h_ref[r : r + 256, :], w_ref[...], 1, 0).astype(BF16)
    lane_head = lax.broadcasted_iota(jnp.int32, (1, cols), 1) // HEAD
    for first in range(0, total_rows, block):
        end = first + block
        q = qkv_ref[first:end, 0:cols] * jnp.asarray(HEAD**-0.5, BF16)
        k = qkv_ref[0:end, cols : 2 * cols]
        v = qkv_ref[0:end, 2 * cols : 3 * cols]
        start = starts(lengths, hi, first + lax.broadcasted_iota(jnp.int32, (block, 1), 0))
        row = first + lax.broadcasted_iota(jnp.int32, (block, end), 0)
        col = lax.broadcasted_iota(jnp.int32, (block, end), 1)
        permit = (col <= row) & (col >= start)
        out = jnp.zeros((block, cols), F32)
        lane = lax.broadcasted_iota(jnp.int32, (block, 128), 1)
        lse = jnp.zeros((block, 128), F32)
        for h in range(heads):
            qh = jnp.where(lane_head == h, q, jnp.zeros_like(q))
            s = jnp.where(permit, dot(qh, k, 1, 1), MASKED)
            top = jnp.max(s, 1, keepdims=True)
            p = jnp.exp(s - top)
            total = jnp.sum(p, 1, keepdims=True)
            o = dot(p.astype(BF16), v, 1, 0) * (1.0 / total)
            out = jnp.where(lane_head == h, o, out)
            lse = jnp.where(lane == h, top + jnp.log(total), lse)
        attn_ref[first:end, :] = out.astype(BF16)
        lse_ref[:, first:end] = lse.T[: lse_ref.shape[0]]
    for m in range(group):
        for kind in (0, 1):
            pieces[m][kind * frames : (kind + 1) * frames, :] = attn_ref[place(kind, m), :]


def attend_back(heads, block, group, frames, meta, lengths, *refs):
    qkv_ref, attn_ref, lse_ref = refs[:3]
    pieces = refs[3 : 3 + group]
    full_ref, keep_ref, send_ref = refs[3 + group : 6 + group]
    do_ref, dk_ref, dv_ref, delta_ref = refs[6 + group :]
    hi, low, core = meta[HI], meta[LOW], meta[CORE]
    total_rows = qkv_ref.shape[0]
    cols = heads * HEAD
    for m in range(group):
        for kind in (0, 1):
            do_ref[rows_at((hi ^ kind) * group + (low ^ m), frames), :] = pieces[m][
                kind * frames : (kind + 1) * frames, :
            ]
    some = lse_ref.shape[0]
    pick = (
        lax.broadcasted_iota(jnp.int32, (some, cols), 1) // HEAD
        == lax.broadcasted_iota(jnp.int32, (some, cols), 0)
    ).astype(F32)
    for r in range(0, total_rows, block):
        product = do_ref[r : r + block, :].astype(F32) * attn_ref[r : r + block, :].astype(F32)
        delta_ref[:, r : r + block] = lax.dot_general(
            pick,
            product,
            (((1,), (1,)), ((), ())),
            precision=lax.Precision.HIGHEST,
            preferred_element_type=F32,
        )
    lane_head = lax.broadcasted_iota(jnp.int32, (1, cols), 1) // HEAD
    scale = HEAD**-0.5
    dk_ref[...] = jnp.zeros_like(dk_ref)
    dv_ref[...] = jnp.zeros_like(dv_ref)
    for first in range(0, total_rows, block):
        end = first + block
        q = qkv_ref[first:end, 0:cols] * jnp.asarray(scale, BF16)
        do = do_ref[first:end, :]
        k = qkv_ref[0:end, cols : 2 * cols]
        v = qkv_ref[0:end, 2 * cols : 3 * cols]
        start = starts(lengths, hi, first + lax.broadcasted_iota(jnp.int32, (1, block), 1))
        row = first + lax.broadcasted_iota(jnp.int32, (end, block), 1)
        col = lax.broadcasted_iota(jnp.int32, (end, block), 0)
        permit = (col <= row) & (col >= start)

        def some_heads(step, carry):
            dq = full_ref[first:end, 0:cols]
            for j in range(min(2, heads)):
                h = step * min(2, heads) + j
                mine = lane_head == h
                qh = jnp.where(mine, q, jnp.zeros_like(q))
                doh = jnp.where(mine, do, jnp.zeros_like(do))
                s = dot(k, qh, 1, 1)
                p = jnp.where(permit, jnp.exp(s - lse_ref[pl.ds(h, 1), first:end]), 0.0)
                dp = dot(v, doh, 1, 1)
                ds = (p * (dp - delta_ref[pl.ds(h, 1), first:end])).astype(BF16)
                dv_ref[0:end, :] += dot(p.astype(BF16), doh, 1, 0)
                dk_ref[0:end, :] += dot(ds, qh, 1, 0)
                dq = jnp.where(mine, (dot(ds, k, 0, 0) * scale).astype(BF16), dq)
            full_ref[first:end, 0:cols] = dq
            return carry

        lax.fori_loop(0, -(-heads // 2), some_heads, 0)
    full_ref[:, cols : 2 * cols] = dk_ref[...].astype(BF16)
    full_ref[:, 2 * cols : 3 * cols] = dv_ref[...].astype(BF16)
    for i in range(2 * group // 2):
        at = slice(i * frames, (i + 1) * frames)
        keep_ref[at, :] = full_ref[rows_at(2 * i + core, frames), :]
        send_ref[at, :] = full_ref[rows_at(2 * i + 1 - core, frames), :]


def mix(group, frames, meta, *refs):
    pieces = refs[:group]
    own_ref, other_ref, w_ref, gain_ref, shift_ref, x2_ref, h_ref = refs[group:]
    cols = pieces[0].shape[1]
    total = None
    for m in range(group):
        part = dot(pieces[m][...], w_ref[rows_at(meta[LOW] ^ m, cols), :], 1, 0)
        total = part if total is None else total + part
    for i, ref in enumerate((own_ref, other_ref)):
        at = slice(i * frames, (i + 1) * frames)
        x2 = ref[...].astype(F32) + total[at]
        x2_ref[at, :] = x2
        h_ref[at, :] = (normal(x2)[0] * gain_ref[...] + shift_ref[...]).astype(BF16)


def masks_without(nb, bit):
    return [m for m in range(nb) if not m & bit]


def split_store(b, bit, nb, tile, keep, send, j):
    masks = masks_without(nb, bit)
    for i in range(nb):
        mask = b ^ i
        low = lax.rem(mask, bit)
        index = low + lax.div(mask, 2 * bit) * bit

        @pl.when(mask & bit == 0)
        def _():
            keep[index, j] = tile(i)

        @pl.when(mask & bit != 0)
        def _():
            send[index, j] = tile(i)


def feed_body(part, parts, group, frames, nb, meta, *refs):
    h_ref, g_ref, wu_ref, bu_ref, wd_ref = refs[:5]
    refs = refs[5:]
    if part > 0:
        out_before, dh_before = refs[:2]
        refs = refs[2:]
    if part == parts - 1:
        x_ref, bd_ref, gain_ref, wo_ref = refs[:4]
        refs = refs[4:]
    act_keep, act_send, pre_keep, pre_send, gbu_ref = refs[:5]
    refs = refs[5:]
    out_acc, dh_acc = refs[-2:]
    step = pl.program_id(0)
    sub = act_keep.shape[3]
    pre = dot(h_ref[...], wu_ref[...], 1, 0) + bu_ref[...]
    square = pre * pre
    t = jnp.tanh(pre * (SQ + (SQ * CUBE) * square))
    half = 0.5 + 0.5 * t
    act = (pre * half).astype(BF16)
    slope = half + 0.5 * pre * (1.0 - t * t) * (SQ + (3 * SQ * CUBE) * square)
    d_pre = (dot(g_ref[...], wd_ref[...], 1, 1) * slope).astype(BF16)
    gbu_ref[...] = jnp.sum(d_pre.astype(F32), 0, keepdims=True)
    for v, bit, keep, send in ((act, 2, act_keep, act_send), (d_pre, 1, pre_keep, pre_send)):
        split_store(meta[B], bit, nb, lambda i: v[:, i * sub : (i + 1) * sub], keep, send, 0)
    out_add = dot(act, wd_ref[...], 1, 0)
    dh_add = dot(d_pre, wu_ref[...], 1, 1)

    @pl.when(step == 0)
    def _():
        if part > 0:
            out_acc[...] = out_before[...] + out_add
            dh_acc[...] = dh_before[...] + dh_add
        else:
            out_acc[...] = out_add
            dh_acc[...] = dh_add

    @pl.when(step > 0)
    def _():
        out_acc[...] += out_add
        dh_acc[...] += dh_add

    if part == parts - 1:
        out_keep, out_send, dx_ref, dy_ref = refs[:4]
        pieces, vec_ref = refs[4 : 4 + group], refs[4 + group]

        @pl.when(step == pl.num_programs(0) - 1)
        def _():
            x2 = x_ref[...]
            out = (x2 + out_acc[...] + bd_ref[...]).astype(BF16)
            out_keep[...] = out[:frames]
            out_send[...] = out[frames:]
            unit, inverse = normal(x2)
            dh = dh_acc[...]
            gf = g_ref[...].astype(F32)
            dx = gf + normal_back(dh * gain_ref[...], unit, inverse)
            dx_ref[...] = dx
            dy = dx.astype(BF16)
            dy_ref[...] = dy
            cols = pieces[0].shape[1]
            for m in range(group):
                pieces[m][...] = dot(dy, wo_ref[rows_at(meta[LOW] ^ m, cols), :], 1, 1).astype(BF16)
            vec_ref[...] = jnp.zeros_like(vec_ref)
            vec_ref[0:1, :] = jnp.sum(dh * unit, 0, keepdims=True)
            vec_ref[1:2, :] = jnp.sum(dh, 0, keepdims=True)
            vec_ref[2:3, :] = jnp.sum(gf, 0, keepdims=True)


def feed(part, parts, deps, before, meta, group, frames, nk, nb, h2, g, x2, w_up, b_up, w_down, b_down, gain, w_out):
    tokens, width = h2.shape
    hidden = w_up.shape[1]
    span = hidden // nk
    steps = nk // parts
    whole = lambda i, meta: (0, 0)
    last = part == parts - 1
    full = pl.BlockSpec((tokens, width), whole)
    row = pl.BlockSpec((1, width), whole)
    block = pl.BlockSpec((nb // 2, 1, tokens, span // nb), lambda i, meta: (0, i, 0, 0))
    args = [h2, g, w_up, b_up[None], w_down] + list(before)
    in_specs = [
        full,
        full,
        pl.BlockSpec((width, span), lambda i, meta: (0, parts * i + part)),
        pl.BlockSpec((1, span), lambda i, meta: (0, parts * i + part)),
        pl.BlockSpec((span, width), lambda i, meta: (parts * i + part, 0)),
    ] + [full] * len(before)
    out_shape = [shape((nb // 2, steps, tokens, span // nb))] * 4 + [shape((1, steps * span), F32)]
    out_specs = [block] * 4 + [pl.BlockSpec((1, span), lambda i, meta: (0, i))]
    scratch = []
    if last:
        args += [x2, b_down[None], gain[None], w_out]
        in_specs += [full, row, row, pl.BlockSpec((width, width), whole)]
        out_shape += [shape((frames, width))] * 2 + [shape((tokens, width), F32), shape((tokens, width))]
        out_shape += [shape((tokens, width // group))] * group + [shape((8, width), F32)]
        out_specs += [pl.BlockSpec((frames, width), whole)] * 2 + [full, full]
        out_specs += [pl.BlockSpec((tokens, width // group), whole)] * group
        out_specs += [pl.BlockSpec((8, width), whole)]
        scratch = [pltpu.VMEM((tokens, width), F32)] * 2
    else:
        out_shape += [shape((tokens, width), F32)] * 2
        out_specs += [full, full]
    ins = len(args) + 1
    return pl.pallas_call(
        lambda *refs: feed_body(part, parts, group, frames, nb, *refs[:ins], *refs[ins + len(deps) :]),
        grid_spec=pltpu.PrefetchScalarGridSpec(
            num_scalar_prefetch=1,
            grid=(steps,),
            in_specs=in_specs + [ANY] * len(deps),
            out_specs=out_specs,
            scratch_shapes=scratch,
        ),
        out_shape=out_shape,
        compiler_params=pltpu.CompilerParams(vmem_limit_bytes=48 * MIB),
        cost_estimate=cost("feed"),
        name="feed",
    )(meta, *args, *deps)


def side_by_side(ref, indices):
    return jnp.concatenate([ref[i, j] for i, j in indices], 1)


def hidden_body(nz, meta, *refs):
    pres, hs, acts, gs = refs[:2], refs[2:4], refs[4:6], refs[6:8]
    keep, send, acc = refs[8:]
    many, _, _, sub = pres[0].shape
    some = nz // 2
    tall, wide = keep.shape[3:]
    half = wide // 2
    width = acc.shape[0]
    core = meta[CORE]
    if sub % 128 == 0:
        span = many * sub

        def up_chip(z, carry):
            part = [
                dot(hs[i][...], side_by_side(pres[i], [(r, z) for r in range(many)]), 0, 0) for i in range(2)
            ]
            acc[:, rows_at(z, span)] = part[0] + part[1]
            return carry

        lax.fori_loop(0, nz, up_chip, 0)
    else:
        for i in range(2):
            order = [(r, z) for z in range(nz) for r in range(many)]
            part = dot(hs[i][...], side_by_side(pres[i], order), 0, 0)
            acc[...] = part if i == 0 else acc[...] + part
    rows = width // nz // 2
    for to, out in ((core, keep), (1 - core, send)):
        mine = acc[:, rows_at(to, some * many * sub)].astype(BF16)
        for r in range(many):
            v = jnp.concatenate([mine[:, (j * many + r) * sub : (j * many + r + 1) * sub] for j in range(some)], 1)
            for z in range(nz):
                for c in range(2):
                    first = (2 * z + c) * rows
                    out[0, r, z ^ meta[Z], :, rows_at(c ^ to, half)] = v[first : first + rows]
    if sub % 128 == 0:

        def down_chip(z, carry):
            part = [
                dot(side_by_side(acts[i], [(r, z) for r in range(many)]), gs[i][...], 0, 0) for i in range(2)
            ]
            part = part[0] + part[1]
            for r in range(many):
                acc[rows_at(r * nz + z, sub), :] = part[r * sub : (r + 1) * sub]
            return carry

        lax.fori_loop(0, nz, down_chip, 0)
    else:
        for i in range(2):
            order = [(r, z) for r in range(many) for z in range(nz)]
            part = dot(side_by_side(acts[i], order), gs[i][...], 0, 0)
            acc[...] = part if i == 0 else acc[...] + part
    fold = tall // sub
    for to, out in ((core, keep), (1 - core, send)):
        for q in range(fold):
            v = acc[:, pl.ds(pl.multiple_of((to * fold + q) * wide, wide), wide)].astype(BF16)
            for r in range(many):
                for z in range(nz):
                    first = (r * nz + z) * sub
                    out[1, r, z ^ meta[Z], q * sub : (q + 1) * sub, :] = v[first : first + sub]


def hidden_cores(keep, got, *outs):
    many = keep.shape[1]
    for i in range(2):
        for r in range(many):
            outs[i * many + r][...] = (keep[i, r].astype(F32) + got[i, r].astype(F32)).astype(BF16)


def hidden_plane(count, *refs):
    ins, refs = refs[: 2 * count], refs[2 * count :]
    nz = ins[0].shape[0]
    more, outs = refs[:-nz], refs[-nz:]
    tall = ins[0].shape[1]
    for i in range(2):
        v = ins[i * count][...].astype(F32)
        for one in ins[i * count + 1 : (i + 1) * count]:
            v = v + one[...].astype(F32)
        for z, out in enumerate(outs):
            out[i * tall : (i + 1) * tall] = v[z].astype(BF16)
    if more:
        v = more[0][0].astype(F32) + more[1][0].astype(F32)
        v = v.astype(BF16).reshape(v.shape[0], 2, -1, ins[0].shape[2])
        small = v.shape[2]
        for z, out in enumerate(outs):
            for c in range(2):
                first = 2 * tall + c * small
                out[first : first + small] = v[z, c]


def sum_of(refs):
    v = refs[0][...].astype(F32)
    for one in refs[1:]:
        v = v + one[...].astype(F32)
    return v.astype(BF16)


def hidden_first(*refs):
    refs[-1][...] = sum_of(refs[:-1])


def hidden_line(meta, *refs):
    first, terms, outs = refs[0], refs[1:-4], refs[-4:]
    tall, wide = outs[0].shape
    half = wide // 2
    downs = []
    for h, v in enumerate((first[...], sum_of(terms))):
        outs[0][:, h * half : (h + 1) * half] = v[:tall, :half]
        outs[1][:, h * half : (h + 1) * half] = v[:tall, half:]
        downs.append(v[tall : 2 * tall])
    mine = meta[CORE] == 0
    outs[2][:tall] = jnp.where(mine, downs[0], downs[1])
    outs[3][:tall] = jnp.where(mine, downs[1], downs[0])
    small = (v.shape[0] - 2 * tall) // 2
    outs[2][tall:] = v[2 * tall : 2 * tall + small]
    outs[3][tall:] = v[2 * tall + small :]


def out_body(group, meta, *refs):
    pieces, dy_ref, keep, send = refs[:group], refs[group], refs[-2], refs[-1]
    nb, _, _, small, half = keep.shape
    for core, out in ((meta[CORE], keep), (1 - meta[CORE], send)):
        dy = dy_ref[:, rows_at(core, half)]
        for m in range(group):
            part = dot(pieces[m][...], dy, 0, 0).astype(BF16)
            for j in range(2):
                for i in range(nb):
                    first = (j * nb + i) * small
                    at = (meta[B] ^ i, meta[LOW] ^ m ^ meta[Z], j ^ core)
                    out[at] = part[first : first + small]


def reverse_bits(v, count):
    out = 0
    for j in range(count):
        out = out + ((v >> j) & 1) * 2 ** (count - 1 - j)
    return out


def qkv_body(meta, h_ref, d_ref, keep, send, acc):
    half, nk, small, _ = keep.shape
    nb = 2 * half
    acc[...] = dot(h_ref[...], d_ref[...], 0, 0)
    for i in range(nb):
        index = reverse_bits(meta[B] ^ i, nb.bit_length() - 1)
        for out, mine in ((keep, index < half), (send, index >= half)):

            @pl.when(mine)
            def _():
                for j in range(nk):
                    first = (j * nb + i) * small
                    out[lax.rem(index, half), j] = acc[first : first + small, :].astype(BF16)


def fold_body(keep, ref, *outs):
    count = ref.shape[0] // keep
    v = ref[:keep].astype(F32)
    for i in range(1, count):
        v = v + ref[i * keep : (i + 1) * keep].astype(F32)
    v = v.astype(BF16)
    for out in outs:
        if len(out.shape) == len(v.shape):
            out[...] = v
        else:
            for i in range(out.shape[0]):
                out[i] = v


def add_body(count, cuts, *refs):
    ins, outs = refs[:count], refs[count:]
    first = 0
    for out, size in zip(outs, cuts):
        v = ins[0][first : first + size].astype(F32)
        for one in ins[1:]:
            v = v + one[first : first + size].astype(F32)
        out[...] = v.astype(out.dtype).reshape(out.shape)
        first = first + size


def stack_body(*refs):
    at = 0
    for ref in refs[:-1]:
        size = ref.shape[0]
        refs[-1][at : at + size] = ref[...]
        at += size


def part_body(group, frames, meta, keep_ref, got_ref, mine_ref, theirs_ref, *refs):
    outs, acc = refs[:-1], refs[-1]
    acc[...] = dot(keep_ref[...], mine_ref[...], 1, 1) + dot(got_ref[...], theirs_ref[...], 1, 1)
    half = group // 2
    for m in range(half):
        for kind in (0, 1):
            first = (meta[HI] ^ kind) * half + (lax.div(meta[LOW], 2) ^ m)
            outs[m][kind * frames : (kind + 1) * frames, :] = acc[rows_at(first, frames), :].astype(
                outs[m].dtype
            )


def final_body(frames, count, *refs):
    terms = refs[:count]
    own_ref, other_ref, dx_ref, gain_ref, keep_ref, send_ref, vec_ref = refs[count:]
    gains = jnp.zeros((1, dx_ref.shape[1]), F32)
    sums = gains
    for i, (ref, out) in enumerate(((own_ref, keep_ref), (other_ref, send_ref))):
        at = slice(i * frames, (i + 1) * frames)
        dh = terms[0][at, :]
        for term in terms[1:]:
            dh = dh + term[at, :].astype(F32)
        unit, inverse = normal(ref[...].astype(F32))
        out[...] = (dx_ref[at, :] + normal_back(dh * gain_ref[...], unit, inverse)).astype(BF16)
        gains = gains + jnp.sum(dh * unit, 0, keepdims=True)
        sums = sums + jnp.sum(dh, 0, keepdims=True)
    vec_ref[...] = jnp.zeros_like(vec_ref)
    vec_ref[0:1, :] = gains
    vec_ref[1:2, :] = sums


def place_down(tall, fold, masks, meta, *refs):
    pieces, out, more = refs[:-2], refs[-2], refs[-1]
    at = 0
    for ref in pieces:
        for i in range(ref.shape[0]):
            rows, cols = tall // fold, ref.shape[3]
            small = ref.shape[2] - tall
            for c in range(2):
                more[rows_at(meta[B] ^ masks[at], small), rows_at(c ^ meta[CORE], cols)] = ref[i, c, tall:].astype(F32)
                for q in range(fold):
                    out[rows_at(meta[B] ^ masks[at], rows), rows_at((c ^ meta[CORE]) * fold + q, cols)] = ref[
                        i, c, q * rows : (q + 1) * rows
                    ].astype(F32)
            at += 1


def place_up(nb, nz, masks, meta, *refs):
    pieces, out = refs[:-1], refs[-1]
    at = 0
    for ref in pieces:
        for i in range(ref.shape[0]):
            some = nz // 2
            sub = ref.shape[3] // nz
            for c in range(2):
                for h in range(2):
                    for j in range(some):
                        chip = (c ^ meta[CORE]) * some + j
                        first = (2 * chip + h) * nb + (meta[B] ^ masks[at])
                        lane = (h * some + j) * sub
                        out[:, rows_at(first, sub)] = ref[i, c, :, lane : lane + sub].astype(F32)
            at += 1


def place_qkv(ref, out):
    nb, group, small, width = ref.shape
    cols = width // 3
    for i in range(nb):
        for l in range(group):
            for j in range(3):
                first = (j * group + l) * cols
                out[i * small : (i + 1) * small, first : first + cols] = ref[
                    i, l, :, j * cols : (j + 1) * cols
                ].astype(F32)


def make(nb, nk):
    nz = nk // 2

    def on_blk(v, mask):
        return lax.ppermute(v, "blk", [(i, i ^ mask) for i in range(nk)])

    def on_batch(v, mask):
        return lax.ppermute(v, "batch", [(i, i ^ mask) for i in range(nb)])

    def on_device(
        tokens, lengths, ln1_gain, ln1_bias, w_qkv, w_out, ln2_gain, ln2_bias,
        w_up, b_up, w_down, b_down, cotangent,
    ):
        _, frames, width = tokens.shape
        hidden = w_up.shape[1]
        group = nk // 2
        heads = HEADS // group
        cols = heads * HEAD
        whole_row = nk * frames
        own = 2 * frames
        some = -(-heads // 8) * 8
        b = lax.axis_index("batch")
        k = lax.axis_index("blk")
        z, core = k // 2, k % 2
        hi, low = k // group, k % group
        meta = jnp.stack([hi, low, core, z, b, b, b, b]).astype(jnp.int32)

        def pick(v, index):
            return lax.dynamic_index_in_dim(v, index, 0, keepdims=False)

        before = []

        def kernel(body, outs, args, *rest, deps=(), **kw):
            result = call(body, outs, args, *rest, deps=list(deps) + before, **kw)
            before[:] = [min(result[: len(outs)], key=lambda v: v.size)]
            return result

        mine = {0: pick(tokens, hi)}
        other = {0: on_blk(pick(tokens, 1 - hi), group)}
        def choose(meta, v, keep, send):
            keep[...] = v[meta[HI]]
            send[...] = v[1 - meta[HI]]

        cot_mine, cot_send = kernel(
            choose,
            [shape((frames, width))] * 2,
            [meta, cotangent],
            1,
            deps=[other[0]],
            name="cotangent",
        )
        m = group // 2
        while m >= 1:
            for v in (mine, other):
                for key in list(v):
                    v[key ^ m] = on_blk(v[key], m)
            m //= 2
        mine = [mine[m] for m in range(group)]
        other = [other[m] for m in range(group)]

        def head_weights(which):
            parts = [
                lax.dynamic_slice_in_dim(w_qkv, i * width + which * cols, cols, 1) for i in range(3)
            ]
            return jnp.concatenate(parts, 1)

        w_mine, w_theirs = head_weights(low), head_weights(low ^ 1)

        h_row, qkv, attn_heads, lse, *pieces = kernel(
            lambda *refs: attend_rows(heads, 256, group, frames, *refs),
            [
                shape((whole_row, width)),
                shape((whole_row, 3 * cols)),
                shape((whole_row, cols)),
                shape((some, whole_row), F32),
            ]
            + [shape((own, cols))] * group,
            [meta, lengths] + mine + other + [w_mine, ln1_gain[None], ln1_bias[None]],
            scalars=2,
            name="attend_rows",
        )
        attn = [pieces[0]] + [on_blk(pieces[m], m) for m in range(1, group)]

        def join(a, c, out):
            out[:frames] = a[...]
            out[frames:] = c[...]

        (g,) = kernel(join, [shape((own, width))], [cot_mine, on_blk(cot_send, group)], name="join")
        g_other = on_batch(g, 2)
        x2, h2 = kernel(
            lambda *refs: mix(group, frames, *refs),
            [shape((own, width), F32), shape((own, width))],
            [meta] + attn + [mine[0], other[0], w_out, ln2_gain[None], ln2_bias[None]],
            scalars=1,
            name="mix",
        )
        h2_other = on_batch(h2, 1)
        feed_args = (meta, group, frames, nk, nb, h2, g, x2, w_up, b_up, w_down, b_down, ln2_gain, w_out)
        act_keep, act_send, pre_keep, pre_send, gbu_0, *rest = feed(0, 2, before + [g_other], (), *feed_args)
        hidden_0 = [pre_keep, on_batch(pre_send, 1), h2, h2_other, act_keep, on_batch(act_send, 2), g, g_other]
        act_keep, act_send, pre_keep, pre_send, gbu_1, out_keep, out_send, d_x2, d_y, *rest = feed(
            1, 2, [h2_other], rest, *feed_args
        )
        pieces, vec2 = rest[:group], rest[group]
        before[:] = [vec2]
        d_heads = [pieces[0]] + [on_blk(pieces[m], m) for m in range(1, group)]
        hidden_1 = [pre_keep, on_batch(pre_send, 1), h2, h2_other, act_keep, on_batch(act_send, 2), g, g_other]

        rows = width // nk
        small = rows // nb
        sub = hidden // nk // nb
        half = width // 2
        simple = small % 8 == 0 and sub % 128 == 0 and cols % 128 == 0
        bits = [2**j for j in range(nb.bit_length() - 1)]

        def add(arrays, cuts, drop=True, name="add", deps=()):
            rest = arrays[0].shape[1:]
            outs = [shape(rest if size == 1 and drop else (size,) + rest) for size in cuts]
            return kernel(lambda *refs: add_body(len(arrays), cuts, *refs), outs, list(arrays), name=name, deps=deps)

        def plane(v):
            return lax.all_to_all(v, "batch", 0, 0, tiled=True)

        def line(v):
            return lax.all_to_all(v, "blk", 0, 0, tiled=True)

        wide = hidden // 2 // nb

        def hidden_grad(args, **kw):
            keep, send = kernel(
                lambda *refs: hidden_body(nz, *refs),
                [shape((2, nb // 2, nz, rows, wide))] * 2,
                [meta] + args,
                scalars=1,
                scratch=[pltpu.VMEM((width, width), F32)],
                name="hidden_grad",
                **kw,
            )
            return keep, on_blk(send, 1)

        def hidden_cores_sum(keep, got, **kw):
            parts = kernel(hidden_cores, [shape((nz, rows, wide))] * nb, [keep, got], name="hidden_cores", **kw)
            half = nb // 2
            ups = [on_batch(v, m) for v, m in zip(parts[1:half], masks_without(nb, 1)[1:])]
            downs = [on_batch(v, m) for v, m in zip(parts[half + 1 :], masks_without(nb, 2)[1:])]
            return [parts[0]] + ups + [parts[half]] + downs

        extra = small * half // wide

        def hidden_plane_sum(terms, more=()):
            tall = 2 * rows + (2 * extra if more else 0)
            parts = kernel(
                lambda *refs: hidden_plane(nb // 2, *refs),
                [shape((tall, wide))] * nz,
                list(terms) + list(more),
                name="hidden_plane",
            )
            return [parts[0]] + [on_blk(parts[m], 2 * m) for m in range(1, nz)]

        def out_halve(keep, got, deps=()):
            size = keep.shape[0]
            return add([keep, got], [size // 2, size // 2], drop=False, name="out_sum", deps=deps)

        hidden_0 = hidden_grad(hidden_0)
        hidden_0 = hidden_cores_sum(*hidden_0)
        hidden_1 = hidden_grad(hidden_1, deps=d_heads[1:])
        hidden_1 = hidden_cores_sum(*hidden_1)
        hidden_0 = hidden_plane_sum(hidden_0)
        d_qkv, keep, send = kernel(
            lambda *refs: attend_back(heads, 256, group, frames, *refs),
            [shape((whole_row, 3 * cols))] + [shape((whole_row // 2, 3 * cols))] * 2,
            [meta, lengths, qkv, attn_heads, lse] + d_heads,
            scalars=2,
            scratch=[
                pltpu.VMEM((whole_row, cols), BF16),
                pltpu.VMEM((whole_row, cols), F32),
                pltpu.VMEM((whole_row, cols), F32),
                pltpu.VMEM((some, whole_row), F32),
            ],
            name="attend_back",
        )
        got = on_blk(send, 1)
        if simple:
            qkv_keep, qkv_send = kernel(
                qkv_body,
                [shape((nb // 2, nk, small, 3 * cols))] * 2,
                [meta, h_row, d_qkv],
                scalars=1,
                scratch=[pltpu.VMEM((width, 3 * cols), F32)],
                name="qkv_grad",
                deps=[hidden_1[nb // 2 - 1], hidden_1[-1]],
            )
        else:
            w = dot(h_row, d_qkv, 0, 0).astype(BF16).reshape(nk, nb, small, 3 * cols)
            order = [reverse_bits(i, len(bits)) for i in range(nb)]
            w = w[:, b ^ jnp.array(order)].transpose(1, 0, 2, 3)
            qkv_keep, qkv_send = w[: nb // 2], w[nb // 2 :]

        if simple:
            keep_out, send_out = kernel(
                lambda *refs: out_body(group, *refs),
                [shape((nb, nz, 2, small, half))] * 2,
                [meta] + attn + [d_y],
                scalars=1,
                name="out_grad",
            )
        else:
            w = jnp.stack([dot(one, d_y, 0, 0) for one in attn]).astype(BF16)[low ^ jnp.arange(group)]
            w = w.reshape(nz, 2, nb, small, 2, half).transpose(4, 2, 0, 1, 3, 5)
            w = w[core ^ jnp.arange(2)][:, b ^ jnp.arange(nb)][:, :, z ^ jnp.arange(nz)]
            w = w[:, :, :, core ^ jnp.arange(2)]
            keep_out, send_out = w[0], w[1][:, :, ::-1]

        out_got = on_blk(send_out, 1)
        qkv_got = on_batch(qkv_send, bits[0])
        out_keep2, out_send2 = out_halve(keep_out, out_got)
        out_got = on_batch(out_send2, bits[-1])
        terms = kernel(
            lambda *refs: part_body(group, frames, *refs),
            [shape((own, width), F32)] + [shape((own, width))] * (group // 2 - 1),
            [meta, keep, got, w_mine, w_theirs],
            scalars=1,
            scratch=[pltpu.VMEM((whole_row // 2, width), F32)],
            name="part",
        )
        terms = [terms[0]] + [on_blk(terms[m], 2 * m) for m in range(1, group // 2)]
        for mask in bits[-2::-1]:
            out_keep2, out_send2 = out_halve(out_keep2, out_got)
            out_got = on_batch(out_send2, mask)
        (first,) = kernel(hidden_first, [shape((2 * rows, wide))], hidden_0, name="hidden_first")
        hidden_1 = hidden_plane_sum(hidden_1, [out_keep2, out_got])

        def halve(keep, got):
            size = keep.shape[0]
            if size == 1:
                return add([keep, got], [1], name="qkv_sum")
            return add([keep, got], [size // 2, size // 2], drop=False, name="qkv_sum")

        for mask in bits[1:]:
            qkv_keep, qkv_send = halve(qkv_keep, qkv_got)
            qkv_got = on_batch(qkv_send, mask)
        keep, send, vec1 = kernel(
            lambda *refs: final_body(frames, len(terms), *refs),
            [shape((frames, width))] * 2 + [shape((8, width), F32)],
            list(terms) + [mine[0], other[0], d_x2, ln1_gain[None]],
            name="final",
            deps=[qkv_got],
        )
        (part,) = halve(qkv_keep, qkv_got)
        part = line(part)
        vec = jnp.concatenate(
            [vec1[:2].reshape(-1, 128), vec2[:3].reshape(-1, 128)]
            + [gbu_0.reshape(-1, 128), gbu_1.reshape(-1, 128)],
            0,
        )
        masks = [(on_blk, 2**j) for j in range(nk.bit_length() - 1)] + [(on_batch, m) for m in bits]

        def vec_move():
            move, mask = masks.pop(0)
            return move(vec, mask)

        def vec_add(got, **kw):
            (v,) = kernel(
                lambda *refs: add_body(2, [vec.shape[0]], *refs), [shape(vec.shape, F32)], [vec, got], name="vec", **kw
            )
            return v

        vec_got = vec_move()
        up_keep, up_send, down_keep, down_send = kernel(
            hidden_line,
            [shape((rows, wide))] * 2 + [shape((rows + extra, wide))] * 2,
            [meta, first] + hidden_1,
            1,
            name="hidden_line",
            deps=[vec_got],
        )
        vec = vec_add(vec_got)
        up_got, down_got = on_blk(up_send, 1), on_blk(down_send, 1)

        def pair_up(meta, keep, got, out):
            out[meta[HI]] = keep[...]
            out[1 - meta[HI]] = got[...]

        def two_rows(keep, got):
            (v,) = kernel(pair_up, [shape((2, frames, width))], [meta, keep, got], 1, name="pair")
            return v

        grad_got = on_blk(send, group)
        grad_keep = keep
        def stack(pieces, deps=()):
            if len(pieces) == 1:
                return pieces[0]
            size = sum(one.shape[0] for one in pieces)
            (v,) = kernel(
                stack_body, [shape((size,) + pieces[0].shape[1:])], list(pieces), name="stack", deps=deps
            )
            return v

        vec_got = vec_move()
        up = [stack([up_keep[None], up_got[None]], deps=[down_got, vec_got])[None]]
        down = [stack([down_keep[None], down_got[None]])[None]]
        vec = vec_add(vec_got)
        up_order, down_order = [0], [0]
        out_got = on_blk(out_send, group)
        for mask_up, mask_down in zip(bits, bits[::-1]):
            if len(up_order) == 2:
                vec_got = vec_move()
                up = [stack(up, deps=[down[-1], vec_got])]
                down = [stack(down)]
                (qkvs,) = kernel(
                    lambda *refs: fold_body(group, *refs),
                    [shape((nb, group, small, 3 * cols))],
                    [part],
                    name="qkv_line",
                )
                qkvs = plane(qkvs)
                vec = vec_add(vec_got)
            elif len(up_order) > 2:
                up = [stack(up, deps=[down[-1]])]
                down = [stack(down)]
            up, up_order = [up[0], on_batch(up[0], mask_up)], up_order + [mask_up ^ one for one in up_order]
            down, down_order = (
                [down[0], on_batch(down[0], mask_down)],
                down_order + [mask_down ^ one for one in down_order],
            )
        while len(masks) > 1:
            vec = vec_add(vec_move())
        vec_got = vec_move()

        if simple:
            (g_w_up,) = kernel(
                lambda *refs: place_up(nb, nz, up_order, *refs),
                [shape((rows, hidden), F32)],
                [meta] + up,
                1,
                name="place_up",
            )
            g_w_down, g_w_out = kernel(
                lambda *refs: place_down(rows, rows // sub, down_order, *refs),
                [shape((nb * sub, width), F32), shape((rows, width), F32)],
                [meta] + down,
                1,
                name="place_down",
            )
            (g_w_qkv,) = kernel(
                place_qkv, [shape((rows, 3 * width), F32)], [qkvs], name="place_qkv", deps=[vec_got]
            )
        else:
            both = core ^ jnp.arange(2)

            def in_order(pieces, order):
                back = [order.index(i) for i in range(nb)]
                w = jnp.concatenate(pieces, 0)[jnp.array(back)]
                return w[b ^ jnp.arange(nb)].astype(F32)

            more = in_order(down, down_order)[:, both]
            w = more[:, :, :rows].reshape(nb, 2, rows // sub, sub, wide)
            g_w_down = w.transpose(0, 3, 1, 2, 4).reshape(nb * sub, width)
            w = more[:, :, rows:].reshape(nb, 2, small, half)
            g_w_out = w.transpose(0, 2, 1, 3).reshape(rows, width)
            w = in_order(up, up_order)[:, both].reshape(nb, 2, rows, 2, nz // 2, sub)
            g_w_up = w.transpose(2, 1, 4, 3, 0, 5).reshape(rows, hidden)
            w = qkvs.reshape(nb, group, small, 3, cols).transpose(0, 2, 3, 1, 4)
            g_w_qkv = w.reshape(rows, 3 * width).astype(F32)

        input_grad = two_rows(grad_keep, grad_got)
        output = two_rows(out_keep, out_got)
        per = width // 128
        if nk == per:
            def vec_last(meta, v, got, *outs):
                k = 2 * meta[Z] + meta[CORE]
                for i in range(5):
                    at = pl.ds(i * per + k, 1)
                    outs[i][...] = v[at, :] + got[at, :]
                each = outs[5].shape[0]
                at = pl.ds(5 * per + (meta[CORE] * nz + meta[Z]) * each, each)
                outs[5][...] = v[at, :] + got[at, :]

            shares = kernel(
                vec_last,
                [shape((1, 128), F32)] * 5 + [shape((hidden // nk // 128, 128), F32)],
                [meta, vec, vec_got],
                1,
                name="vec",
            )
            shares = [one.reshape(-1) for one in shares]
        else:
            vec = vec_add(vec_got)

            def share(first, count):
                flat = vec[first : first + count].reshape(-1)
                if first == 5 * per:
                    flat = flat.reshape(2, nz, -1).transpose(1, 0, 2).reshape(-1)
                size = flat.shape[0] // nk
                return lax.dynamic_slice_in_dim(flat, k * size, size, 0)

            shares = [share(i * per, per) for i in range(5)] + [share(5 * per, hidden // 128)]

        return (
            output,
            input_grad,
            shares[0],
            shares[1],
            g_w_qkv,
            g_w_out,
            shares[2],
            shares[3],
            g_w_up,
            shares[5],
            g_w_down,
            shares[4],
        )

    return on_device


def solution(mesh):
    act = P("batch", "blk", None)
    return jax.shard_map(
        make(mesh.shape["batch"], mesh.shape["blk"]),
        mesh=mesh,
        in_specs=(act, P("batch", None)) + (P(),) * 10 + (act,),
        out_specs=(
            act, act, P("blk"), P("blk"), P("blk", None), P("blk", None), P("blk"), P("blk"),
            P("blk", None), P("blk"), P("blk", None), P("blk"),
        ),
        check_vma=False,
    )
```

```python
import jax
import jax.numpy as jnp
from jax import lax
from jax.experimental import pallas as pl
from jax.experimental.pallas import tpu as pltpu
from jax.sharding import PartitionSpec as P

HEADS = 16
HEAD = 64
EPS = 1e-05
MASKED = -1e30
F32 = jnp.float32
BF16 = jnp.bfloat16
SQ = 0.7978845608
CUBE = 0.044715
MIB = 2**20
HI, LOW, CORE, Z, B = range(5)

VMEM = pl.BlockSpec(memory_space=pltpu.VMEM)
SMEM = pl.BlockSpec(memory_space=pltpu.SMEM)
ANY = pl.BlockSpec(memory_space=pl.ANY)
MICROS = {
    "attend_rows": 11, "mix": 1.5, "feed": 10, "attend_back": 10.6, "qkv_grad": 2.5, "part": 3.4, "up_grad": 2.7,
    "down_grad": 2.6, "out_grad": 1.3, "place_up": 2, "place_down": 2, "place_qkv": 2, "place_out": 1.3,
}


def cost(name):
    return pl.CostEstimate(flops=int(2e9 * MICROS.get(name, 0.7)), bytes_accessed=0, transcendentals=0)


def dot(a, b, ca, cb):
    return lax.dot_general(a, b, (((ca,), (cb,)), ((), ())), preferred_element_type=F32)


def shape(dims, kind=BF16):
    return jax.ShapeDtypeStruct(tuple(dims), kind)


def call(body, outs, args, scalars=0, scratch=(), name=None, limit=48, deps=(), through=()):
    ins, count = len(args), len(outs)
    last = ins + len(deps) + len(through)
    done = last + count + len(through)
    return pl.pallas_call(
        lambda *refs: body(*refs[:ins], *refs[last : last + count], *refs[done:]),
        in_specs=[SMEM] * scalars + [VMEM] * (ins - scalars) + [ANY] * (len(deps) + len(through)),
        out_specs=tuple(VMEM for _ in outs) + tuple(ANY for _ in through),
        out_shape=tuple(outs) + tuple(shape(v.shape, v.dtype) for v in through),
        input_output_aliases={ins + len(deps) + i: count + i for i in range(len(through))},
        scratch_shapes=list(scratch),
        compiler_params=pltpu.CompilerParams(vmem_limit_bytes=limit * MIB),
        cost_estimate=cost(name),
        name=name,
    )(*args, *deps, *through)


def rows_at(index, size):
    return pl.ds(pl.multiple_of(index * size, size), size)


def normal(x):
    mean = jnp.mean(x, -1, keepdims=True)
    centred = x - mean
    inverse = lax.rsqrt(jnp.mean(centred * centred, -1, keepdims=True) + EPS)
    return centred * inverse, inverse


def normal_back(scaled, unit, inverse):
    return inverse * (
        scaled
        - jnp.mean(scaled, -1, keepdims=True)
        - unit * jnp.mean(scaled * unit, -1, keepdims=True)
    )


def starts(lengths_ref, hi, place):
    start = jnp.zeros_like(place)
    end = jnp.int32(0)
    for j in range(lengths_ref.shape[1]):
        size = lengths_ref[hi, j]
        end = end + size
        start = jnp.where(place >= end, end, start)
    return start


def attend_rows(heads, block, group, frames, meta, lengths, *refs):
    own, other = refs[:group], refs[group : 2 * group]
    w_ref, gain_ref, shift_ref = refs[2 * group : 2 * group + 3]
    h_ref, qkv_ref, attn_ref, lse_ref = refs[2 * group + 3 : 2 * group + 7]
    pieces = refs[2 * group + 7 :]
    hi, low = meta[HI], meta[LOW]
    cols = heads * HEAD
    total_rows = h_ref.shape[0]

    def place(kind, m):
        return rows_at((hi ^ kind) * group + (low ^ m), frames)

    for m in range(group):
        for kind, ref in ((0, own[m]), (1, other[m])):
            unit, _ = normal(ref[...].astype(F32))
            h_ref[place(kind, m), :] = (unit * gain_ref[...] + shift_ref[...]).astype(BF16)
    for r in range(0, total_rows, 256):
        qkv_ref[r : r + 256, :] = dot(h_ref[r : r + 256, :], w_ref[...], 1, 0).astype(BF16)
    lane_head = lax.broadcasted_iota(jnp.int32, (1, cols), 1) // HEAD
    for first in range(0, total_rows, block):
        end = first + block
        q = qkv_ref[first:end, 0:cols] * jnp.asarray(HEAD**-0.5, BF16)
        k = qkv_ref[0:end, cols : 2 * cols]
        v = qkv_ref[0:end, 2 * cols : 3 * cols]
        start = starts(lengths, hi, first + lax.broadcasted_iota(jnp.int32, (block, 1), 0))
        row = first + lax.broadcasted_iota(jnp.int32, (block, end), 0)
        col = lax.broadcasted_iota(jnp.int32, (block, end), 1)
        permit = (col <= row) & (col >= start)
        out = jnp.zeros((block, cols), F32)
        lane = lax.broadcasted_iota(jnp.int32, (block, 128), 1)
        lse = jnp.zeros((block, 128), F32)
        for h in range(heads):
            qh = jnp.where(lane_head == h, q, jnp.zeros_like(q))
            s = jnp.where(permit, dot(qh, k, 1, 1), MASKED)
            top = jnp.max(s, 1, keepdims=True)
            p = jnp.exp(s - top)
            total = jnp.sum(p, 1, keepdims=True)
            o = dot(p.astype(BF16), v, 1, 0) * (1.0 / total)
            out = jnp.where(lane_head == h, o, out)
            lse = jnp.where(lane == h, top + jnp.log(total), lse)
        attn_ref[first:end, :] = out.astype(BF16)
        lse_ref[:, first:end] = lse.T[: lse_ref.shape[0]]
    for m in range(group):
        for kind in (0, 1):
            pieces[m][kind * frames : (kind + 1) * frames, :] = attn_ref[place(kind, m), :]


def attend_back(heads, block, group, frames, meta, lengths, *refs):
    qkv_ref, attn_ref, lse_ref = refs[:3]
    pieces = refs[3 : 3 + group]
    full_ref, keep_ref, send_ref = refs[3 + group : 6 + group]
    do_ref, dk_ref, dv_ref, delta_ref = refs[6 + group :]
    hi, low, core = meta[HI], meta[LOW], meta[CORE]
    total_rows = qkv_ref.shape[0]
    cols = heads * HEAD
    for m in range(group):
        for kind in (0, 1):
            do_ref[rows_at((hi ^ kind) * group + (low ^ m), frames), :] = pieces[m][
                kind * frames : (kind + 1) * frames, :
            ]
    some = lse_ref.shape[0]
    pick = (
        lax.broadcasted_iota(jnp.int32, (some, cols), 1) // HEAD
        == lax.broadcasted_iota(jnp.int32, (some, cols), 0)
    ).astype(F32)
    for r in range(0, total_rows, block):
        product = do_ref[r : r + block, :].astype(F32) * attn_ref[r : r + block, :].astype(F32)
        delta_ref[:, r : r + block] = lax.dot_general(
            pick,
            product,
            (((1,), (1,)), ((), ())),
            precision=lax.Precision.HIGHEST,
            preferred_element_type=F32,
        )
    lane_head = lax.broadcasted_iota(jnp.int32, (1, cols), 1) // HEAD
    scale = HEAD**-0.5
    dk_ref[...] = jnp.zeros_like(dk_ref)
    dv_ref[...] = jnp.zeros_like(dv_ref)
    for first in range(0, total_rows, block):
        end = first + block
        q = qkv_ref[first:end, 0:cols] * jnp.asarray(scale, BF16)
        do = do_ref[first:end, :]
        k = qkv_ref[0:end, cols : 2 * cols]
        v = qkv_ref[0:end, 2 * cols : 3 * cols]
        start = starts(lengths, hi, first + lax.broadcasted_iota(jnp.int32, (1, block), 1))
        row = first + lax.broadcasted_iota(jnp.int32, (end, block), 1)
        col = lax.broadcasted_iota(jnp.int32, (end, block), 0)
        permit = (col <= row) & (col >= start)

        def some_heads(step, carry):
            dq = full_ref[first:end, 0:cols]
            for j in range(min(2, heads)):
                h = step * min(2, heads) + j
                mine = lane_head == h
                qh = jnp.where(mine, q, jnp.zeros_like(q))
                doh = jnp.where(mine, do, jnp.zeros_like(do))
                s = dot(k, qh, 1, 1)
                p = jnp.where(permit, jnp.exp(s - lse_ref[pl.ds(h, 1), first:end]), 0.0)
                dp = dot(v, doh, 1, 1)
                ds = (p * (dp - delta_ref[pl.ds(h, 1), first:end])).astype(BF16)
                dv_ref[0:end, :] += dot(p.astype(BF16), doh, 1, 0)
                dk_ref[0:end, :] += dot(ds, qh, 1, 0)
                dq = jnp.where(mine, (dot(ds, k, 0, 0) * scale).astype(BF16), dq)
            full_ref[first:end, 0:cols] = dq
            return carry

        lax.fori_loop(0, -(-heads // 2), some_heads, 0)
    full_ref[:, cols : 2 * cols] = dk_ref[...].astype(BF16)
    full_ref[:, 2 * cols : 3 * cols] = dv_ref[...].astype(BF16)
    for i in range(2 * group // 2):
        at = slice(i * frames, (i + 1) * frames)
        keep_ref[at, :] = full_ref[rows_at(2 * i + core, frames), :]
        send_ref[at, :] = full_ref[rows_at(2 * i + 1 - core, frames), :]


def mix(group, frames, meta, *refs):
    pieces = refs[:group]
    own_ref, other_ref, w_ref, gain_ref, shift_ref, x2_ref, h_ref = refs[group:]
    cols = pieces[0].shape[1]
    total = None
    for m in range(group):
        part = dot(pieces[m][...], w_ref[rows_at(meta[LOW] ^ m, cols), :], 1, 0)
        total = part if total is None else total + part
    for i, ref in enumerate((own_ref, other_ref)):
        at = slice(i * frames, (i + 1) * frames)
        x2 = ref[...].astype(F32) + total[at]
        x2_ref[at, :] = x2
        h_ref[at, :] = (normal(x2)[0] * gain_ref[...] + shift_ref[...]).astype(BF16)


def masks_without(nb, bit):
    return [m for m in range(nb) if not m & bit]


def split_store(b, bit, nb, tile, keep, send, j):
    masks = masks_without(nb, bit)
    for i in range(nb):
        mask = b ^ i
        low = lax.rem(mask, bit)
        index = low + lax.div(mask, 2 * bit) * bit

        @pl.when(mask & bit == 0)
        def _():
            keep[index, j] = tile(i)

        @pl.when(mask & bit != 0)
        def _():
            send[index, j] = tile(i)


def feed_body(part, parts, group, frames, nb, meta, *refs):
    h_ref, g_ref, wu_ref, bu_ref, wd_ref = refs[:5]
    refs = refs[5:]
    if part > 0:
        out_before, dh_before = refs[:2]
        refs = refs[2:]
    if part == parts - 1:
        x_ref, bd_ref, gain_ref, wo_ref = refs[:4]
        refs = refs[4:]
    act_keep, act_send, pre_keep, pre_send, gbu_ref = refs[:5]
    refs = refs[5:]
    out_acc, dh_acc = refs[-2:]
    step = pl.program_id(0)
    sub = act_keep.shape[3]
    pre = dot(h_ref[...], wu_ref[...], 1, 0) + bu_ref[...]
    square = pre * pre
    t = jnp.tanh(pre * (SQ + (SQ * CUBE) * square))
    half = 0.5 + 0.5 * t
    act = (pre * half).astype(BF16)
    slope = half + 0.5 * pre * (1.0 - t * t) * (SQ + (3 * SQ * CUBE) * square)
    d_pre = (dot(g_ref[...], wd_ref[...], 1, 1) * slope).astype(BF16)
    gbu_ref[...] = jnp.sum(d_pre.astype(F32), 0, keepdims=True)
    for v, bit, keep, send in ((act, 2, act_keep, act_send), (d_pre, 1, pre_keep, pre_send)):
        split_store(meta[B], bit, nb, lambda i: v[:, i * sub : (i + 1) * sub], keep, send, 0)
    out_add = dot(act, wd_ref[...], 1, 0)
    dh_add = dot(d_pre, wu_ref[...], 1, 1)

    @pl.when(step == 0)
    def _():
        if part > 0:
            out_acc[...] = out_before[...] + out_add
            dh_acc[...] = dh_before[...] + dh_add
        else:
            out_acc[...] = out_add
            dh_acc[...] = dh_add

    @pl.when(step > 0)
    def _():
        out_acc[...] += out_add
        dh_acc[...] += dh_add

    if part == parts - 1:
        out_keep, out_send, dx_ref, dy_ref = refs[:4]
        pieces, vec_ref = refs[4 : 4 + group], refs[4 + group]

        @pl.when(step == pl.num_programs(0) - 1)
        def _():
            x2 = x_ref[...]
            out = (x2 + out_acc[...] + bd_ref[...]).astype(BF16)
            out_keep[...] = out[:frames]
            out_send[...] = out[frames:]
            unit, inverse = normal(x2)
            dh = dh_acc[...]
            gf = g_ref[...].astype(F32)
            dx = gf + normal_back(dh * gain_ref[...], unit, inverse)
            dx_ref[...] = dx
            dy = dx.astype(BF16)
            dy_ref[...] = dy
            cols = pieces[0].shape[1]
            for m in range(group):
                pieces[m][...] = dot(dy, wo_ref[rows_at(meta[LOW] ^ m, cols), :], 1, 1).astype(BF16)
            vec_ref[...] = jnp.zeros_like(vec_ref)
            vec_ref[0:1, :] = jnp.sum(dh * unit, 0, keepdims=True)
            vec_ref[1:2, :] = jnp.sum(dh, 0, keepdims=True)
            vec_ref[2:3, :] = jnp.sum(gf, 0, keepdims=True)


def feed(part, parts, deps, before, meta, group, frames, nk, nb, h2, g, x2, w_up, b_up, w_down, b_down, gain, w_out):
    tokens, width = h2.shape
    hidden = w_up.shape[1]
    span = hidden // nk
    steps = nk // parts
    whole = lambda i, meta: (0, 0)
    last = part == parts - 1
    full = pl.BlockSpec((tokens, width), whole)
    row = pl.BlockSpec((1, width), whole)
    block = pl.BlockSpec((nb // 2, 1, tokens, span // nb), lambda i, meta: (0, i, 0, 0))
    args = [h2, g, w_up, b_up[None], w_down] + list(before)
    in_specs = [
        full,
        full,
        pl.BlockSpec((width, span), lambda i, meta: (0, parts * i + part)),
        pl.BlockSpec((1, span), lambda i, meta: (0, parts * i + part)),
        pl.BlockSpec((span, width), lambda i, meta: (parts * i + part, 0)),
    ] + [full] * len(before)
    out_shape = [shape((nb // 2, steps, tokens, span // nb))] * 4 + [shape((1, steps * span), F32)]
    out_specs = [block] * 4 + [pl.BlockSpec((1, span), lambda i, meta: (0, i))]
    scratch = []
    if last:
        args += [x2, b_down[None], gain[None], w_out]
        in_specs += [full, row, row, pl.BlockSpec((width, width), whole)]
        out_shape += [shape((frames, width))] * 2 + [shape((tokens, width), F32), shape((tokens, width))]
        out_shape += [shape((tokens, width // group))] * group + [shape((8, width), F32)]
        out_specs += [pl.BlockSpec((frames, width), whole)] * 2 + [full, full]
        out_specs += [pl.BlockSpec((tokens, width // group), whole)] * group
        out_specs += [pl.BlockSpec((8, width), whole)]
        scratch = [pltpu.VMEM((tokens, width), F32)] * 2
    else:
        out_shape += [shape((tokens, width), F32)] * 2
        out_specs += [full, full]
    ins = len(args) + 1
    return pl.pallas_call(
        lambda *refs: feed_body(part, parts, group, frames, nb, *refs[:ins], *refs[ins + len(deps) :]),
        grid_spec=pltpu.PrefetchScalarGridSpec(
            num_scalar_prefetch=1,
            grid=(steps,),
            in_specs=in_specs + [ANY] * len(deps),
            out_specs=out_specs,
            scratch_shapes=scratch,
        ),
        out_shape=out_shape,
        compiler_params=pltpu.CompilerParams(vmem_limit_bytes=48 * MIB),
        cost_estimate=cost("feed"),
        name="feed",
    )(meta, *args, *deps)


def side_by_side(ref, indices):
    return jnp.concatenate([ref[i, j] for i, j in indices], 1)


def hidden_body(nz, meta, *refs):
    pres, hs, acts, gs = refs[:2], refs[2:4], refs[4:6], refs[6:8]
    keep, send, acc = refs[8:]
    many, _, _, sub = pres[0].shape
    some = nz // 2
    tall, wide = keep.shape[3:]
    half = wide // 2
    width = acc.shape[0]
    core = meta[CORE]
    if sub % 128 == 0:
        span = many * sub

        def up_chip(z, carry):
            part = [
                dot(hs[i][...], side_by_side(pres[i], [(r, z) for r in range(many)]), 0, 0) for i in range(2)
            ]
            acc[:, rows_at(z, span)] = part[0] + part[1]
            return carry

        lax.fori_loop(0, nz, up_chip, 0)
    else:
        for i in range(2):
            order = [(r, z) for z in range(nz) for r in range(many)]
            part = dot(hs[i][...], side_by_side(pres[i], order), 0, 0)
            acc[...] = part if i == 0 else acc[...] + part
    rows = width // nz // 2
    for to, out in ((core, keep), (1 - core, send)):
        mine = acc[:, rows_at(to, some * many * sub)].astype(BF16)
        for r in range(many):
            v = jnp.concatenate([mine[:, (j * many + r) * sub : (j * many + r + 1) * sub] for j in range(some)], 1)
            for z in range(nz):
                for c in range(2):
                    first = (2 * z + c) * rows
                    out[0, r, z ^ meta[Z], :, rows_at(c ^ to, half)] = v[first : first + rows]
    if sub % 128 == 0:

        def down_chip(z, carry):
            part = [
                dot(side_by_side(acts[i], [(r, z) for r in range(many)]), gs[i][...], 0, 0) for i in range(2)
            ]
            part = part[0] + part[1]
            for r in range(many):
                acc[rows_at(r * nz + z, sub), :] = part[r * sub : (r + 1) * sub]
            return carry

        lax.fori_loop(0, nz, down_chip, 0)
    else:
        for i in range(2):
            order = [(r, z) for r in range(many) for z in range(nz)]
            part = dot(side_by_side(acts[i], order), gs[i][...], 0, 0)
            acc[...] = part if i == 0 else acc[...] + part
    fold = tall // sub
    for to, out in ((core, keep), (1 - core, send)):
        for q in range(fold):
            v = acc[:, pl.ds(pl.multiple_of((to * fold + q) * wide, wide), wide)].astype(BF16)
            for r in range(many):
                for z in range(nz):
                    first = (r * nz + z) * sub
                    out[1, r, z ^ meta[Z], q * sub : (q + 1) * sub, :] = v[first : first + sub]


def hidden_cores(keep, got, *outs):
    many = keep.shape[1]
    for i in range(2):
        for r in range(many):
            outs[i * many + r][...] = (keep[i, r].astype(F32) + got[i, r].astype(F32)).astype(BF16)


def hidden_plane(count, *refs):
    ins, refs = refs[: 2 * count], refs[2 * count :]
    nz = ins[0].shape[0]
    more, outs = refs[:-nz], refs[-nz:]
    tall = ins[0].shape[1]
    for i in range(2):
        v = ins[i * count][...].astype(F32)
        for one in ins[i * count + 1 : (i + 1) * count]:
            v = v + one[...].astype(F32)
        for z, out in enumerate(outs):
            out[i * tall : (i + 1) * tall] = v[z].astype(BF16)
    if more:
        v = more[0][0].astype(F32) + more[1][0].astype(F32)
        v = v.astype(BF16).reshape(v.shape[0], 2, -1, ins[0].shape[2])
        small = v.shape[2]
        for z, out in enumerate(outs):
            for c in range(2):
                first = 2 * tall + c * small
                out[first : first + small] = v[z, c]


def sum_of(refs):
    v = refs[0][...].astype(F32)
    for one in refs[1:]:
        v = v + one[...].astype(F32)
    return v.astype(BF16)


def hidden_first(*refs):
    refs[-1][...] = sum_of(refs[:-1])


def hidden_line(meta, *refs):
    first, terms, outs = refs[0], refs[1:-4], refs[-4:]
    tall, wide = outs[0].shape
    half = wide // 2
    downs = []
    for h, v in enumerate((first[...], sum_of(terms))):
        outs[0][:, h * half : (h + 1) * half] = v[:tall, :half]
        outs[1][:, h * half : (h + 1) * half] = v[:tall, half:]
        downs.append(v[tall : 2 * tall])
    mine = meta[CORE] == 0
    outs[2][:tall] = jnp.where(mine, downs[0], downs[1])
    outs[3][:tall] = jnp.where(mine, downs[1], downs[0])
    small = (v.shape[0] - 2 * tall) // 2
    outs[2][tall:] = v[2 * tall : 2 * tall + small]
    outs[3][tall:] = v[2 * tall + small :]


def out_body(group, meta, *refs):
    pieces, dy_ref, keep, send = refs[:group], refs[group], refs[-2], refs[-1]
    nb, _, _, small, half = keep.shape
    for core, out in ((meta[CORE], keep), (1 - meta[CORE], send)):
        dy = dy_ref[:, rows_at(core, half)]
        for m in range(group):
            part = dot(pieces[m][...], dy, 0, 0).astype(BF16)
            for j in range(2):
                for i in range(nb):
                    first = (j * nb + i) * small
                    at = (meta[B] ^ i, meta[LOW] ^ m ^ meta[Z], j ^ core)
                    out[at] = part[first : first + small]


def reverse_bits(v, count):
    out = 0
    for j in range(count):
        out = out + ((v >> j) & 1) * 2 ** (count - 1 - j)
    return out


def qkv_body(meta, h_ref, d_ref, keep, send, acc):
    half, nk, small, _ = keep.shape
    nb = 2 * half
    acc[...] = dot(h_ref[...], d_ref[...], 0, 0)
    for i in range(nb):
        index = reverse_bits(meta[B] ^ i, nb.bit_length() - 1)
        for out, mine in ((keep, index < half), (send, index >= half)):

            @pl.when(mine)
            def _():
                for j in range(nk):
                    first = (j * nb + i) * small
                    out[lax.rem(index, half), j] = acc[first : first + small, :].astype(BF16)


def fold_body(keep, ref, *outs):
    count = ref.shape[0] // keep
    v = ref[:keep].astype(F32)
    for i in range(1, count):
        v = v + ref[i * keep : (i + 1) * keep].astype(F32)
    v = v.astype(BF16)
    for out in outs:
        if len(out.shape) == len(v.shape):
            out[...] = v
        else:
            for i in range(out.shape[0]):
                out[i] = v


def add_body(count, cuts, *refs):
    ins, outs = refs[:count], refs[count:]
    first = 0
    for out, size in zip(outs, cuts):
        v = ins[0][first : first + size].astype(F32)
        for one in ins[1:]:
            v = v + one[first : first + size].astype(F32)
        out[...] = v.astype(out.dtype).reshape(out.shape)
        first = first + size


def stack_body(*refs):
    at = 0
    for ref in refs[:-1]:
        size = ref.shape[0]
        refs[-1][at : at + size] = ref[...]
        at += size


def part_body(group, frames, meta, keep_ref, got_ref, mine_ref, theirs_ref, *refs):
    outs, acc = refs[:-1], refs[-1]
    acc[...] = dot(keep_ref[...], mine_ref[...], 1, 1) + dot(got_ref[...], theirs_ref[...], 1, 1)
    half = group // 2
    for m in range(half):
        for kind in (0, 1):
            first = (meta[HI] ^ kind) * half + (lax.div(meta[LOW], 2) ^ m)
            outs[m][kind * frames : (kind + 1) * frames, :] = acc[rows_at(first, frames), :].astype(
                outs[m].dtype
            )


def final_body(frames, count, *refs):
    terms = refs[:count]
    own_ref, other_ref, dx_ref, gain_ref, keep_ref, send_ref, vec_ref = refs[count:]
    gains = jnp.zeros((1, dx_ref.shape[1]), F32)
    sums = gains
    for i, (ref, out) in enumerate(((own_ref, keep_ref), (other_ref, send_ref))):
        at = slice(i * frames, (i + 1) * frames)
        dh = terms[0][at, :]
        for term in terms[1:]:
            dh = dh + term[at, :].astype(F32)
        unit, inverse = normal(ref[...].astype(F32))
        out[...] = (dx_ref[at, :] + normal_back(dh * gain_ref[...], unit, inverse)).astype(BF16)
        gains = gains + jnp.sum(dh * unit, 0, keepdims=True)
        sums = sums + jnp.sum(dh, 0, keepdims=True)
    vec_ref[...] = jnp.zeros_like(vec_ref)
    vec_ref[0:1, :] = gains
    vec_ref[1:2, :] = sums


def place_down(tall, fold, masks, meta, *refs):
    pieces, out, more = refs[:-2], refs[-2], refs[-1]
    at = 0
    for ref in pieces:
        for i in range(ref.shape[0]):
            rows, cols = tall // fold, ref.shape[3]
            small = ref.shape[2] - tall
            for c in range(2):
                more[rows_at(meta[B] ^ masks[at], small), rows_at(c ^ meta[CORE], cols)] = ref[i, c, tall:].astype(F32)
                for q in range(fold):
                    out[rows_at(meta[B] ^ masks[at], rows), rows_at((c ^ meta[CORE]) * fold + q, cols)] = ref[
                        i, c, q * rows : (q + 1) * rows
                    ].astype(F32)
            at += 1


def place_up(nb, nz, masks, meta, *refs):
    pieces, out = refs[:-1], refs[-1]
    at = 0
    for ref in pieces:
        for i in range(ref.shape[0]):
            some = nz // 2
            sub = ref.shape[3] // nz
            for c in range(2):
                for h in range(2):
                    for j in range(some):
                        chip = (c ^ meta[CORE]) * some + j
                        first = (2 * chip + h) * nb + (meta[B] ^ masks[at])
                        lane = (h * some + j) * sub
                        out[:, rows_at(first, sub)] = ref[i, c, :, lane : lane + sub].astype(F32)
            at += 1


def place_qkv(ref, out):
    nb, group, small, width = ref.shape
    cols = width // 3
    for i in range(nb):
        for l in range(group):
            for j in range(3):
                first = (j * group + l) * cols
                out[i * small : (i + 1) * small, first : first + cols] = ref[
                    i, l, :, j * cols : (j + 1) * cols
                ].astype(F32)


def make(nb, nk):
    nz = nk // 2

    def on_blk(v, mask):
        return lax.ppermute(v, "blk", [(i, i ^ mask) for i in range(nk)])

    def on_batch(v, mask):
        return lax.ppermute(v, "batch", [(i, i ^ mask) for i in range(nb)])

    def on_device(
        tokens, lengths, ln1_gain, ln1_bias, w_qkv, w_out, ln2_gain, ln2_bias,
        w_up, b_up, w_down, b_down, cotangent,
    ):
        _, frames, width = tokens.shape
        hidden = w_up.shape[1]
        group = nk // 2
        heads = HEADS // group
        cols = heads * HEAD
        whole_row = nk * frames
        own = 2 * frames
        some = -(-heads // 8) * 8
        b = lax.axis_index("batch")
        k = lax.axis_index("blk")
        z, core = k // 2, k % 2
        hi, low = k // group, k % group
        meta = jnp.stack([hi, low, core, z, b, b, b, b]).astype(jnp.int32)

        def pick(v, index):
            return lax.dynamic_index_in_dim(v, index, 0, keepdims=False)

        before = []

        def kernel(body, outs, args, *rest, deps=(), **kw):
            result = call(body, outs, args, *rest, deps=list(deps) + before, **kw)
            before[:] = [min(result[: len(outs)], key=lambda v: v.size)]
            return result

        mine = {0: pick(tokens, hi)}
        other = {0: on_blk(pick(tokens, 1 - hi), group)}
        def choose(meta, v, keep, send):
            keep[...] = v[meta[HI]]
            send[...] = v[1 - meta[HI]]

        cot_mine, cot_send = kernel(
            choose,
            [shape((frames, width))] * 2,
            [meta, cotangent],
            1,
            deps=[other[0]],
            name="cotangent",
        )
        m = group // 2
        while m >= 1:
            for v in (mine, other):
                for key in list(v):
                    v[key ^ m] = on_blk(v[key], m)
            m //= 2
        mine = [mine[m] for m in range(group)]
        other = [other[m] for m in range(group)]

        def head_weights(which):
            parts = [
                lax.dynamic_slice_in_dim(w_qkv, i * width + which * cols, cols, 1) for i in range(3)
            ]
            return jnp.concatenate(parts, 1)

        w_mine, w_theirs = head_weights(low), head_weights(low ^ 1)

        h_row, qkv, attn_heads, lse, *pieces = kernel(
            lambda *refs: attend_rows(heads, 256, group, frames, *refs),
            [
                shape((whole_row, width)),
                shape((whole_row, 3 * cols)),
                shape((whole_row, cols)),
                shape((some, whole_row), F32),
            ]
            + [shape((own, cols))] * group,
            [meta, lengths] + mine + other + [w_mine, ln1_gain[None], ln1_bias[None]],
            scalars=2,
            name="attend_rows",
        )
        attn = [pieces[0]] + [on_blk(pieces[m], m) for m in range(1, group)]

        def join(a, c, out):
            out[:frames] = a[...]
            out[frames:] = c[...]

        (g,) = kernel(join, [shape((own, width))], [cot_mine, on_blk(cot_send, group)], name="join")
        g_other = on_batch(g, 2)
        x2, h2 = kernel(
            lambda *refs: mix(group, frames, *refs),
            [shape((own, width), F32), shape((own, width))],
            [meta] + attn + [mine[0], other[0], w_out, ln2_gain[None], ln2_bias[None]],
            scalars=1,
            name="mix",
        )
        h2_other = on_batch(h2, 1)
        feed_args = (meta, group, frames, nk, nb, h2, g, x2, w_up, b_up, w_down, b_down, ln2_gain, w_out)
        act_keep, act_send, pre_keep, pre_send, gbu_0, *rest = feed(0, 2, before + [g_other], (), *feed_args)
        hidden_0 = [pre_keep, on_batch(pre_send, 1), h2, h2_other, act_keep, on_batch(act_send, 2), g, g_other]
        act_keep, act_send, pre_keep, pre_send, gbu_1, out_keep, out_send, d_x2, d_y, *rest = feed(
            1, 2, [h2_other], rest, *feed_args
        )
        pieces, vec2 = rest[:group], rest[group]
        before[:] = [vec2]
        d_heads = [pieces[0]] + [on_blk(pieces[m], m) for m in range(1, group)]
        hidden_1 = [pre_keep, on_batch(pre_send, 1), h2, h2_other, act_keep, on_batch(act_send, 2), g, g_other]

        rows = width // nk
        small = rows // nb
        sub = hidden // nk // nb
        half = width // 2
        simple = small % 8 == 0 and sub % 128 == 0 and cols % 128 == 0
        bits = [2**j for j in range(nb.bit_length() - 1)]

        def add(arrays, cuts, drop=True, name="add", deps=()):
            rest = arrays[0].shape[1:]
            outs = [shape(rest if size == 1 and drop else (size,) + rest) for size in cuts]
            return kernel(lambda *refs: add_body(len(arrays), cuts, *refs), outs, list(arrays), name=name, deps=deps)

        def plane(v):
            return lax.all_to_all(v, "batch", 0, 0, tiled=True)

        def line(v):
            return lax.all_to_all(v, "blk", 0, 0, tiled=True)

        wide = hidden // 2 // nb

        def hidden_grad(args, **kw):
            keep, send = kernel(
                lambda *refs: hidden_body(nz, *refs),
                [shape((2, nb // 2, nz, rows, wide))] * 2,
                [meta] + args,
                scalars=1,
                scratch=[pltpu.VMEM((width, width), F32)],
                name="hidden_grad",
                **kw,
            )
            return keep, on_blk(send, 1)

        def hidden_cores_sum(keep, got, **kw):
            parts = kernel(hidden_cores, [shape((nz, rows, wide))] * nb, [keep, got], name="hidden_cores", **kw)
            half = nb // 2
            ups = [on_batch(v, m) for v, m in zip(parts[1:half], masks_without(nb, 1)[1:])]
            downs = [on_batch(v, m) for v, m in zip(parts[half + 1 :], masks_without(nb, 2)[1:])]
            return [parts[0]] + ups + [parts[half]] + downs

        extra = small * half // wide

        def hidden_plane_sum(terms, more=()):
            tall = 2 * rows + (2 * extra if more else 0)
            parts = kernel(
                lambda *refs: hidden_plane(nb // 2, *refs),
                [shape((tall, wide))] * nz,
                list(terms) + list(more),
                name="hidden_plane",
            )
            return [parts[0]] + [on_blk(parts[m], 2 * m) for m in range(1, nz)]

        def out_halve(keep, got, deps=()):
            size = keep.shape[0]
            return add([keep, got], [size // 2, size // 2], drop=False, name="out_sum", deps=deps)

        hidden_0 = hidden_grad(hidden_0)
        hidden_0 = hidden_cores_sum(*hidden_0)
        hidden_1 = hidden_grad(hidden_1, deps=d_heads[1:])
        hidden_1 = hidden_cores_sum(*hidden_1)
        hidden_0 = hidden_plane_sum(hidden_0)
        d_qkv, keep, send = kernel(
            lambda *refs: attend_back(heads, 256, group, frames, *refs),
            [shape((whole_row, 3 * cols))] + [shape((whole_row // 2, 3 * cols))] * 2,
            [meta, lengths, qkv, attn_heads, lse] + d_heads,
            scalars=2,
            scratch=[
                pltpu.VMEM((whole_row, cols), BF16),
                pltpu.VMEM((whole_row, cols), F32),
                pltpu.VMEM((whole_row, cols), F32),
                pltpu.VMEM((some, whole_row), F32),
            ],
            name="attend_back",
        )
        got = on_blk(send, 1)
        if simple:
            qkv_keep, qkv_send = kernel(
                qkv_body,
                [shape((nb // 2, nk, small, 3 * cols))] * 2,
                [meta, h_row, d_qkv],
                scalars=1,
                scratch=[pltpu.VMEM((width, 3 * cols), F32)],
                name="qkv_grad",
                deps=[hidden_1[nb // 2 - 1], hidden_1[-1]],
            )
        else:
            w = dot(h_row, d_qkv, 0, 0).astype(BF16).reshape(nk, nb, small, 3 * cols)
            order = [reverse_bits(i, len(bits)) for i in range(nb)]
            w = w[:, b ^ jnp.array(order)].transpose(1, 0, 2, 3)
            qkv_keep, qkv_send = w[: nb // 2], w[nb // 2 :]

        if simple:
            keep_out, send_out = kernel(
                lambda *refs: out_body(group, *refs),
                [shape((nb, nz, 2, small, half))] * 2,
                [meta] + attn + [d_y],
                scalars=1,
                name="out_grad",
            )
        else:
            w = jnp.stack([dot(one, d_y, 0, 0) for one in attn]).astype(BF16)[low ^ jnp.arange(group)]
            w = w.reshape(nz, 2, nb, small, 2, half).transpose(4, 2, 0, 1, 3, 5)
            w = w[core ^ jnp.arange(2)][:, b ^ jnp.arange(nb)][:, :, z ^ jnp.arange(nz)]
            w = w[:, :, :, core ^ jnp.arange(2)]
            keep_out, send_out = w[0], w[1][:, :, ::-1]

        out_got = on_blk(send_out, 1)
        qkv_got = on_batch(qkv_send, bits[0])
        out_keep2, out_send2 = out_halve(keep_out, out_got)
        out_got = on_batch(out_send2, bits[-1])
        terms = kernel(
            lambda *refs: part_body(group, frames, *refs),
            [shape((own, width), F32)] + [shape((own, width))] * (group // 2 - 1),
            [meta, keep, got, w_mine, w_theirs],
            scalars=1,
            scratch=[pltpu.VMEM((whole_row // 2, width), F32)],
            name="part",
        )
        terms = [terms[0]] + [on_blk(terms[m], 2 * m) for m in range(1, group // 2)]
        for mask in bits[-2::-1]:
            out_keep2, out_send2 = out_halve(out_keep2, out_got)
            out_got = on_batch(out_send2, mask)
        (first,) = kernel(hidden_first, [shape((2 * rows, wide))], hidden_0, name="hidden_first")
        hidden_1 = hidden_plane_sum(hidden_1, [out_keep2, out_got])

        def halve(keep, got):
            size = keep.shape[0]
            if size == 1:
                return add([keep, got], [1], name="qkv_sum")
            return add([keep, got], [size // 2, size // 2], drop=False, name="qkv_sum")

        for mask in bits[1:]:
            qkv_keep, qkv_send = halve(qkv_keep, qkv_got)
            qkv_got = on_batch(qkv_send, mask)
        keep, send, vec1 = kernel(
            lambda *refs: final_body(frames, len(terms), *refs),
            [shape((frames, width))] * 2 + [shape((8, width), F32)],
            list(terms) + [mine[0], other[0], d_x2, ln1_gain[None]],
            name="final",
            deps=[qkv_got],
        )
        (part,) = halve(qkv_keep, qkv_got)
        part = line(part)
        vec = jnp.concatenate(
            [vec1[:2].reshape(-1, 128), vec2[:3].reshape(-1, 128)]
            + [gbu_0.reshape(-1, 128), gbu_1.reshape(-1, 128)],
            0,
        )
        masks = [(on_blk, 2**j) for j in range(nk.bit_length() - 1)] + [(on_batch, m) for m in bits]

        def vec_move():
            move, mask = masks.pop(0)
            return move(vec, mask)

        def vec_add(got, **kw):
            (v,) = kernel(
                lambda *refs: add_body(2, [vec.shape[0]], *refs), [shape(vec.shape, F32)], [vec, got], name="vec", **kw
            )
            return v

        vec_got = vec_move()
        up_keep, up_send, down_keep, down_send = kernel(
            hidden_line,
            [shape((rows, wide))] * 2 + [shape((rows + extra, wide))] * 2,
            [meta, first] + hidden_1,
            1,
            name="hidden_line",
            deps=[vec_got],
        )
        vec = vec_add(vec_got)
        up_got, down_got = on_blk(up_send, 1), on_blk(down_send, 1)

        def pair_up(meta, keep, got, out):
            out[meta[HI]] = keep[...]
            out[1 - meta[HI]] = got[...]

        def two_rows(keep, got):
            (v,) = kernel(pair_up, [shape((2, frames, width))], [meta, keep, got], 1, name="pair")
            return v

        grad_got = on_blk(send, group)
        grad_keep = keep
        def stack(pieces, deps=()):
            if len(pieces) == 1:
                return pieces[0]
            size = sum(one.shape[0] for one in pieces)
            (v,) = kernel(
                stack_body, [shape((size,) + pieces[0].shape[1:])], list(pieces), name="stack", deps=deps
            )
            return v

        vec_got = vec_move()
        up = [stack([up_keep[None], up_got[None]], deps=[down_got, vec_got])[None]]
        down = [stack([down_keep[None], down_got[None]])[None]]
        vec = vec_add(vec_got)
        up_order, down_order = [0], [0]
        out_got = on_blk(out_send, group)
        for mask_up, mask_down in zip(bits, bits[::-1]):
            if len(up_order) == 2:
                vec_got = vec_move()
                up = [stack(up, deps=[down[-1], vec_got])]
                down = [stack(down)]
                (qkvs,) = kernel(
                    lambda *refs: fold_body(group, *refs),
                    [shape((nb, group, small, 3 * cols))],
                    [part],
                    name="qkv_line",
                )
                qkvs = plane(qkvs)
                vec = vec_add(vec_got)
            elif len(up_order) > 2:
                up = [stack(up, deps=[down[-1]])]
                down = [stack(down)]
            up, up_order = [up[0], on_batch(up[0], mask_up)], up_order + [mask_up ^ one for one in up_order]
            down, down_order = (
                [down[0], on_batch(down[0], mask_down)],
                down_order + [mask_down ^ one for one in down_order],
            )
        while len(masks) > 1:
            vec = vec_add(vec_move())
        vec_got = vec_move()

        if simple:
            (g_w_up,) = kernel(
                lambda *refs: place_up(nb, nz, up_order, *refs),
                [shape((rows, hidden), F32)],
                [meta] + up,
                1,
                name="place_up",
            )
            g_w_down, g_w_out = kernel(
                lambda *refs: place_down(rows, rows // sub, down_order, *refs),
                [shape((nb * sub, width), F32), shape((rows, width), F32)],
                [meta] + down,
                1,
                name="place_down",
            )
            (g_w_qkv,) = kernel(
                place_qkv, [shape((rows, 3 * width), F32)], [qkvs], name="place_qkv", deps=[vec_got]
            )
        else:
            both = core ^ jnp.arange(2)

            def in_order(pieces, order):
                back = [order.index(i) for i in range(nb)]
                w = jnp.concatenate(pieces, 0)[jnp.array(back)]
                return w[b ^ jnp.arange(nb)].astype(F32)

            more = in_order(down, down_order)[:, both]
            w = more[:, :, :rows].reshape(nb, 2, rows // sub, sub, wide)
            g_w_down = w.transpose(0, 3, 1, 2, 4).reshape(nb * sub, width)
            w = more[:, :, rows:].reshape(nb, 2, small, half)
            g_w_out = w.transpose(0, 2, 1, 3).reshape(rows, width)
            w = in_order(up, up_order)[:, both].reshape(nb, 2, rows, 2, nz // 2, sub)
            g_w_up = w.transpose(2, 1, 4, 3, 0, 5).reshape(rows, hidden)
            w = qkvs.reshape(nb, group, small, 3, cols).transpose(0, 2, 3, 1, 4)
            g_w_qkv = w.reshape(rows, 3 * width).astype(F32)

        input_grad = two_rows(grad_keep, grad_got)
        output = two_rows(out_keep, out_got)
        per = width // 128
        if nk == per:
            def vec_last(meta, v, got, *outs):
                k = 2 * meta[Z] + meta[CORE]
                for i in range(5):
                    at = pl.ds(i * per + k, 1)
                    outs[i][...] = v[at, :] + got[at, :]
                each = outs[5].shape[0]
                at = pl.ds(5 * per + (meta[CORE] * nz + meta[Z]) * each, each)
                outs[5][...] = v[at, :] + got[at, :]

            shares = kernel(
                vec_last,
                [shape((1, 128), F32)] * 5 + [shape((hidden // nk // 128, 128), F32)],
                [meta, vec, vec_got],
                1,
                name="vec",
            )
            shares = [one.reshape(-1) for one in shares]
        else:
            vec = vec_add(vec_got)

            def share(first, count):
                flat = vec[first : first + count].reshape(-1)
                if first == 5 * per:
                    flat = flat.reshape(2, nz, -1).transpose(1, 0, 2).reshape(-1)
                size = flat.shape[0] // nk
                return lax.dynamic_slice_in_dim(flat, k * size, size, 0)

            shares = [share(i * per, per) for i in range(5)] + [share(5 * per, hidden // 128)]

        return (
            output,
            input_grad,
            shares[0],
            shares[1],
            g_w_qkv,
            g_w_out,
            shares[2],
            shares[3],
            g_w_up,
            shares[5],
            g_w_down,
            shares[4],
        )

    return on_device


def solution(mesh):
    act = P("batch", "blk", None)
    return jax.shard_map(
        make(mesh.shape["batch"], mesh.shape["blk"]),
        mesh=mesh,
        in_specs=(act, P("batch", None)) + (P(),) * 10 + (act,),
        out_specs=(
            act, act, P("blk"), P("blk"), P("blk", None), P("blk", None), P("blk"), P("blk"),
            P("blk", None), P("blk"), P("blk", None), P("blk"),
        ),
        check_vma=False,
    )
```
